128 devices in a mesh: nodes: 8 (over x, core), feat: 16 (over z, y).
Axes of the slice: x: 4, y: 4, z: 4, core: 2. Of those that a mesh axis runs over, the one named last changes fastest.
Arguments:
- node_states: float32 [2, 128, 16384], P(None, 'feat', 'nodes'), may hold values from -6 to 6
- weights: bfloat16 [2, 2, 128, 128], replicated, may hold values from -0.5 to 0.5
- adj_tiles: bfloat16 [128, 4, 128, 128], P('nodes'), may hold values from -0.25 to 0.25
- tile_source: int32 [128, 4], P('nodes'), may hold values from 0 to 31
- tile_count: int32 [128], P('nodes'), may hold values from 1 to 4, as said below
- send_rows: int32 [8, 8, 256], P('nodes'), may hold values from 0 to 2047
- send_count: int32 [8, 8], P('nodes'), may hold values from 1 to 256, as said below
- out_grads: float32 [2, 128, 16384], P(None, 'feat', 'nodes'), may hold values from -6 to 6
Outputs:
- outputs: float32 [2, 128, 16384], P(None, 'feat', 'nodes')
- state_grads: float32 [2, 128, 16384], P(None, 'feat', 'nodes')
- weight_grads: float32 [2, 2, 128, 128], P(None, None, None, 'feat')
The draws below stay inside these ranges and needn't reach their ends.
Inputs may be any that keep to these rules, and one draw needn't show every extreme that they name: `tile_count`: live slots of a destination block; some block holds 4. `send_count`: rows a sender sends to a receiver; every device sends 256 to one receiver and receives 256 from one sender.
All inputs are finite; a program needn't handle non-finite values.
Results may differ from the reference program's by a relative error of at most 0.015.
Values may be sent and summed in bfloat16 or wider, within the bound.
A program may use at most 64 MiB of HBM per device.

```python
import jax
import jax.numpy as jnp
from jax import lax

GROUP_WIDTH = 128
TILE = 128
MAX_BLOCKS = 4
LAYERS = 2
ROWS_DEV = 2048
HALO_SLOTS = 256
NODES = 16384
HALO_ROWS = 2048
SRC_TILES = 32
N_NODES = 8


def draw_tile_count(key, part):
    key = jax.random.fold_in(key, 11)
    first, second = jax.random.split(key)
    blocks = NODES // TILE
    counts = jax.random.randint(first, (blocks,), 1, MAX_BLOCKS + 1, dtype=jnp.int32)
    full_at = jax.random.randint(second, (), 0, blocks, dtype=jnp.int32)
    return jnp.where(jnp.arange(blocks, dtype=jnp.int32) == full_at, MAX_BLOCKS, counts).astype(jnp.int32)


def draw_send_count(key, part):
    key = jax.random.fold_in(key, 23)
    first, second = jax.random.split(key)
    counts = jax.random.randint(first, (N_NODES, N_NODES), 1, HALO_SLOTS + 1, dtype=jnp.int32)
    shift_by = jax.random.randint(second, (), 0, N_NODES, dtype=jnp.int32)
    senders = jnp.arange(N_NODES, dtype=jnp.int32)[:, None]
    receivers = jnp.arange(N_NODES, dtype=jnp.int32)[None, :]
    full = receivers == (senders + shift_by) % N_NODES
    return jnp.where(full, HALO_SLOTS, counts).astype(jnp.int32)


def with_ends(drawn, rng, low, high):
    spot = [jax.random.randint(jax.random.fold_in(rng, axis), (), 0, length) for axis, length in enumerate(drawn.shape)]
    widest = drawn.shape.index(max(drawn.shape))
    neighbour = spot[:widest] + [(spot[widest] + 1) % drawn.shape[widest]] + spot[widest + 1:]
    return drawn.at[tuple(spot)].set(low).at[tuple(neighbour)].set(high)


def shard_levels(stream_key, dims, shards, least, high):
    factor_of = 1.0
    for position, blocks in shards:
        draws = jax.random.uniform(jax.random.fold_in(jax.random.fold_in(stream_key, 6), position), (blocks,), jnp.float32, least / len(shards), high / len(shards))
        factor_of = factor_of * jnp.repeat(jnp.exp(draws), dims[position] // blocks).reshape((-1,) + (1,) * (len(dims) - 1 - position))
    return factor_of


def centred(key, extent, scale, limit, cuts=(), kind=jnp.bfloat16):
    level = shard_levels(key, extent, cuts, -0.22, 0.18) if cuts else 1.0
    values = jax.random.normal(key, extent, jnp.float32) * scale * level
    return jnp.minimum(jnp.maximum(values, -limit), limit).astype(kind)


def setup_inputs(seed: int = 0) -> dict:
    splits = jax.random.split(jax.random.key(seed), 9)
    return {
        "node_states": centred(splits[0], (2, GROUP_WIDTH, NODES), 1.0, 6.0, ((1, 16), (2, 8)), jnp.float32),
        "weights": centred(splits[1], (LAYERS, 2, GROUP_WIDTH, GROUP_WIDTH), GROUP_WIDTH ** -0.5, 0.5),
        "adj_tiles": centred(splits[2], (NODES // TILE, MAX_BLOCKS, TILE, TILE), (MAX_BLOCKS * TILE) ** -0.5, 0.25, ((0, 8),)),
        "tile_source": with_ends(jax.random.randint(splits[3], (NODES // TILE, MAX_BLOCKS), 0, SRC_TILES), jax.random.fold_in(splits[3], 1), 0, SRC_TILES - 1).astype(jnp.int32),
        "tile_count": draw_tile_count(jax.random.fold_in(splits[8], 71), 0),
        "send_rows": with_ends(jax.random.randint(splits[5], (N_NODES, N_NODES, HALO_SLOTS), 0, ROWS_DEV), jax.random.fold_in(splits[5], 1), 0, ROWS_DEV - 1).astype(jnp.int32),
        "send_count": draw_send_count(jax.random.fold_in(splits[8], 71), 0),
        "out_grads": centred(splits[7], (2, GROUP_WIDTH, NODES), 1.0, 6.0, ((1, 16), (2, 8)), jnp.float32),
    }


EPS = 1e-05

def moments(states):
    width = states.shape[0]
    center = lax.optimization_barrier(jnp.sum(states, axis=0)) / width
    spread = lax.optimization_barrier(jnp.sum(states * states, axis=0)) / width - center * center
    inverse = lax.rsqrt(spread + EPS)
    return ((states - center) * inverse, inverse)

def halo_plan(send_rows, send_count):
    offsets = (jnp.arange(N_NODES, dtype=jnp.int32) * ROWS_DEV)[:, None, None]
    where_from = jnp.transpose(offsets + send_rows, (1, 0, 2)).reshape(N_NODES, N_NODES * HALO_SLOTS)
    live = jnp.arange(HALO_SLOTS, dtype=jnp.int32)[None, None, :] < send_count[:, :, None]
    live = jnp.transpose(live, (1, 0, 2)).reshape(N_NODES, N_NODES * HALO_SLOTS)
    return (where_from, live)

def device_tiles(device, graph):
    adj_tiles, tile_source, tile_count, where_from, live = graph
    per_device = ROWS_DEV // TILE
    first = device * per_device
    values = lax.dynamic_slice_in_dim(adj_tiles, first, per_device, 0)
    sources = lax.dynamic_slice_in_dim(tile_source, first, per_device, 0)
    counts = lax.dynamic_slice_in_dim(tile_count, first, per_device, 0)
    keep = jnp.arange(MAX_BLOCKS, dtype=jnp.int32)[None, :] < counts[:, None]
    values = jnp.where(keep[:, :, None, None], values, jnp.zeros((), jnp.bfloat16))
    return (values, sources)

def branch(states, weight, graph):
    where_from, live = (graph[3], graph[4])
    normed, inverse = moments(states)
    activ = jax.nn.silu(normed).astype(jnp.bfloat16)
    mixed = jnp.dot(weight.T, activ, preferred_element_type=jnp.float32).astype(jnp.bfloat16)
    width = mixed.shape[0]
    rim_pad = jnp.zeros((width, HALO_ROWS - N_NODES * HALO_SLOTS), jnp.bfloat16)

    def one_device(device):
        values, sources = device_tiles(device, graph)
        local = lax.dynamic_slice_in_dim(mixed, device * ROWS_DEV, ROWS_DEV, 1)
        rim = jnp.where(live[device][None, :], jnp.take(mixed, where_from[device], axis=1), jnp.zeros((), jnp.bfloat16))
        source = jnp.concatenate([local, rim, rim_pad], axis=1).reshape(width, -1, TILE)[:, sources]
        result = jnp.einsum('jtkc,tkrc->jtr', source.astype(jnp.float32), values.astype(jnp.float32))
        return result.reshape(width, ROWS_DEV)
    result = lax.map(one_device, jnp.arange(N_NODES, dtype=jnp.int32))
    return jnp.transpose(result, (1, 0, 2)).reshape(width, -1)

def branch_grad(states, grad, weight, graph):
    where_from, live = (graph[3], graph[4])
    normed, inverse = moments(states)
    activ = jax.nn.silu(normed).astype(jnp.bfloat16)
    width = grad.shape[0]
    grad_low = grad.astype(jnp.bfloat16)

    def one_device(device):
        values, sources = device_tiles(device, graph)
        block = lax.dynamic_slice_in_dim(grad_low, device * ROWS_DEV, ROWS_DEV, 1).reshape(width, -1, TILE)
        terms = jnp.einsum('jtr,tkrc->jtkc', block.astype(jnp.float32), values.astype(jnp.float32))
        source = jnp.zeros((width, SRC_TILES, TILE), jnp.float32).at[:, sources].add(terms).reshape(width, -1)
        return (source[:, :ROWS_DEV], source[:, ROWS_DEV:ROWS_DEV + N_NODES * HALO_SLOTS].astype(jnp.bfloat16))
    local, rim = lax.map(one_device, jnp.arange(N_NODES, dtype=jnp.int32))
    grad_mixed = jnp.transpose(local, (1, 0, 2)).reshape(width, -1)
    rim = jnp.where(live[:, None, :], rim, jnp.zeros((), jnp.bfloat16)).astype(jnp.float32)
    rim = jnp.transpose(rim, (1, 0, 2)).reshape(width, -1)
    grad_mixed = grad_mixed.at[:, where_from.reshape(-1)].add(rim).astype(jnp.bfloat16)
    weight_grad = jnp.dot(activ, grad_mixed.T, preferred_element_type=jnp.float32)
    grad_act = jnp.dot(weight, grad_mixed, preferred_element_type=jnp.float32)
    gate = jax.nn.sigmoid(normed)
    grad_norm = grad_act * gate * (1.0 + normed * (1.0 - gate))
    grad_states = inverse * (grad_norm - lax.optimization_barrier(jnp.sum(grad_norm, axis=0)) / width - normed * lax.optimization_barrier(jnp.sum(grad_norm * normed, axis=0)) / width)
    return (grad_states, weight_grad)

def reference(node_states, weights, adj_tiles, tile_source, tile_count, send_rows, send_count, out_grads):
    where_from, live = halo_plan(send_rows, send_count)
    graph = (adj_tiles, tile_source, tile_count, where_from, live)
    first, second = (node_states[0], node_states[1])
    for layer in range(LAYERS):
        first = first + branch(second, weights[layer, 0], graph)
        second = second + branch(first, weights[layer, 1], graph)
    outputs = jnp.stack([first, second])
    grad_first, grad_second = (out_grads[0], out_grads[1])
    collected = []
    for layer in range(LAYERS - 1, -1, -1):
        second = second - branch(first, weights[layer, 1], graph)
        grad_states, part_second = branch_grad(first, grad_second, weights[layer, 1], graph)
        grad_first = grad_first + grad_states
        first = first - branch(second, weights[layer, 0], graph)
        grad_states, part_first = branch_grad(second, grad_first, weights[layer, 0], graph)
        grad_second = grad_second + grad_states
        collected.append(jnp.stack([part_first, part_second]))
    weight_grads = jnp.stack(collected[::-1])
    return (outputs, jnp.stack([grad_first, grad_second]), weight_grads)
```

```python
import functools

import jax
import jax.numpy as jnp
from jax import lax
from jax.experimental import pallas as pl
from jax.experimental.pallas import tpu as pltpu
from jax.sharding import PartitionSpec as P

MESH = pl.DeviceIdType.MESH
TILE = 128
EPS = 1e-05
F32 = jnp.float32
BF16 = jnp.bfloat16


def dot(a, b):
    return jnp.dot(a, b, preferred_element_type=F32)


def dot_nt(a, b):
    return lax.dot_general(a, b, (((1,), (1,)), ((), ())), preferred_element_type=F32)


def kernel(
    n_nodes, n_feat,
    states_ref, grads_ref, weights_ref, adj_ref, rows_ref,
    source_ref, count_ref, sent_ref, order_ref, keep_ref, last_ref,
    out_ref, sg_ref, wg_ref,
    ag_send, ag_recv, x1, x2, g1, g2, wt,
    fwd_tiles, adj_sorted, pick, spread,
    normed, dgate, activ, inverse, mixed,
    src0, src1, src2, src3, halo_send, low, segs, rim_send, rim_recv, gm, gml,
    gw_send, gw_recv,
    ag_ss, ag_rs, h_ss, h_rs, r_ss, r_rs, w_ss, w_rs,
):
    src = (src0, src1, src2, src3)
    me_q = lax.axis_index("nodes")
    me_f = lax.axis_index("feat")
    width = states_ref.shape[1]
    rows = states_ref.shape[2]
    total = width * n_feat
    half = rows // 2
    blocks = rows // TILE
    chunks = rows // 256
    depth = adj_ref.shape[1]
    slots = blocks * depth

    def node_peer(d):
        return lax.rem(me_q + d, n_nodes)

    def feat_peer(d):
        return lax.rem(me_f + d, n_feat)

    barrier = pltpu.get_barrier_semaphore()
    for d in range(1, n_feat):
        pl.semaphore_signal(barrier, inc=1, device_id=(me_q, feat_peer(d)), device_id_type=MESH)
    for d in range(1, n_nodes):
        pl.semaphore_signal(barrier, inc=1, device_id=(node_peer(d), me_f), device_id_type=MESH)

    gathered = [(states_ref, 1, x2), (states_ref, 0, x1), (grads_ref, 1, g2), (grads_ref, 0, g1)]
    for a, (ref, group, _) in enumerate(gathered):
        packed = jnp.concatenate([ref[group, :, :half], ref[group, :, half:]], axis=0).astype(BF16)
        ag_send[a] = packed
        ag_recv[a, me_f] = packed
    pl.semaphore_wait(barrier, n_feat - 1 + n_nodes - 1)

    for a in range(len(gathered)):
        for d in range(1, n_feat):
            pltpu.make_async_remote_copy(
                src_ref=ag_send.at[a], dst_ref=ag_recv.at[a, me_f],
                send_sem=ag_ss.at[a], recv_sem=ag_rs.at[a],
                device_id=(me_q, feat_peer(d)), device_id_type=MESH,
            ).start()

    for layer in range(2):
        for group in range(2):
            wt[layer, group] = weights_ref[layer, group].astype(F32).T.astype(BF16)

    def prepare_block(t, _):
        for k in range(depth):
            keep = (k < count_ref[t]).astype(F32)
            tile = adj_ref[t, k].astype(F32) * keep
            fwd_tiles[t, k * TILE:(k + 1) * TILE, :] = tile.T.astype(BF16)
        return 0

    lax.fori_loop(0, blocks, prepare_block, 0)

    def prepare_sorted(i, _):
        e = order_ref[i]
        t = lax.div(e, depth)
        k = lax.rem(e, depth)
        keep = (k < count_ref[t]).astype(F32)
        adj_sorted[i] = (adj_ref[t, k].astype(F32) * keep).astype(BF16)
        return 0

    lax.fori_loop(0, slots, prepare_sorted, 0)

    def prepare_pick(p, _):
        lane = lax.broadcasted_iota(jnp.int32, (1, 256), 1)
        index = jnp.where(lane < sent_ref[0, p], rows_ref[0, pl.ds(p, 1), :], -1)
        high = lax.broadcasted_iota(jnp.int32, (256, 256), 0)
        for c in range(chunks):
            hit = high + c * 256 == index
            pick[p, c * 256:(c + 1) * 256, :] = jnp.where(hit, 1.0, 0.0).astype(BF16)
        value = index.astype(F32)
        place = lax.broadcasted_iota(jnp.int32, (TILE, 256), 1).astype(F32)
        for s in range(2):
            column = jnp.broadcast_to(value[:, s * TILE:(s + 1) * TILE], (TILE, TILE)).T
            column = jnp.concatenate([column, column], axis=1)
            for c in range(chunks):
                hit = place + float(c * 256) == column
                spread[p, s * TILE:(s + 1) * TILE, c * 256:(c + 1) * 256] = jnp.where(hit, 1.0, 0.0).astype(BF16)
        return 0

    lax.fori_loop(0, n_nodes, prepare_pick, 0)

    def take_gathered(a):
        ref, group, target = gathered[a]
        pltpu.make_async_remote_copy(
            src_ref=ag_recv.at[a, pl.ds(0, n_feat - 1)], dst_ref=ag_recv.at[a, pl.ds(0, n_feat - 1)],
            send_sem=ag_ss.at[a], recv_sem=ag_rs.at[a],
            device_id=(me_q, feat_peer(1)), device_id_type=MESH,
        ).wait_recv()
        for f in range(n_feat):
            got = ag_recv[a, f].astype(F32)
            target[f * width:(f + 1) * width, :half] = got[:width]
            target[f * width:(f + 1) * width, half:] = got[width:]
        target[pl.ds(pl.multiple_of(me_f * width, width), width), :] = ref[group]

    def lanes(c, size=256):
        return pl.ds(pl.multiple_of(c * size, size), size)

    def activate(u, b, with_gate):
        def step(c, _):
            states = u[:, lanes(c)]
            center = jnp.sum(states, axis=0, keepdims=True) * (1.0 / total)
            square = jnp.sum(states * states, axis=0, keepdims=True) * (1.0 / total)
            inv = lax.rsqrt(square - center * center + EPS)
            norm = (states - center) * inv
            gate = 1.0 / (1.0 + jnp.exp(-norm))
            normed[b, :, lanes(c)] = norm
            inverse[b, :, lanes(c)] = inv
            activ[b, :, lanes(c)] = (norm * gate).astype(BF16)
            if with_gate:
                dgate[b, :, lanes(c)] = gate * (1.0 + norm * (1.0 - gate))
            return 0

        lax.fori_loop(0, chunks, step, 0)

    def gates(b):
        def step(c, _):
            norm = normed[b, :, lanes(c)]
            gate = 1.0 / (1.0 + jnp.exp(-norm))
            dgate[b, :, lanes(c)] = gate * (1.0 + norm * (1.0 - gate))
            return 0

        lax.fori_loop(0, chunks, step, 0)

    def mix_and_send(b, layer, group):
        def step(c, _):
            value = dot(wt[layer, group], activ[b, :, lanes(c)]).astype(BF16)
            mixed[:, lanes(c)] = value
            src[b][2 * c] = value[:, :TILE]
            src[b][2 * c + 1] = value[:, TILE:]
            return 0

        lax.fori_loop(0, chunks, step, 0)

        def gather(p):
            return dot(mixed[...], pick[p]).astype(BF16)

        def send(i, _):
            p = node_peer(jnp.where(i < 7, i + 1, 0))
            value = gather(p)
            halo_send[b, p, 0] = value[:, :TILE]
            halo_send[b, p, 1] = value[:, TILE:]
            pltpu.make_async_remote_copy(
                src_ref=halo_send.at[b, p], dst_ref=src[b].at[pl.ds(blocks + 2 * me_q, 2)],
                send_sem=h_ss.at[b], recv_sem=h_rs.at[b],
                device_id=(p, me_f), device_id_type=MESH,
            ).start()
            return 0

        lax.fori_loop(0, n_nodes - 1, send, 0)
        value = gather(me_q)
        src[b][blocks + 2 * me_q] = value[:, :TILE]
        src[b][blocks + 2 * me_q + 1] = value[:, TILE:]

    def halo_wait(b):
        here = src[b].at[pl.ds(blocks, 2 * (n_nodes - 1))]
        pltpu.make_async_remote_copy(
            src_ref=here, dst_ref=here, send_sem=h_ss.at[b], recv_sem=h_rs.at[b],
            device_id=(node_peer(1), me_f), device_id_type=MESH,
        ).wait_recv()

    def aggregate(b, u):
        def step(t, _):
            tiles = [src[b][source_ref[t, k]] for k in range(depth)]
            u[:, lanes(t, TILE)] += dot(jnp.concatenate(tiles, axis=1), fwd_tiles[t])
            return 0

        lax.fori_loop(0, blocks, step, 0)

    def rims_and_send(b, g):
        def lower(t, _):
            low[t] = g[:, lanes(t, TILE)].astype(BF16)
            return 0

        lax.fori_loop(0, blocks, lower, 0)

        segs[0] = jnp.zeros((total, TILE), F32)

        def term(i, _):
            part = dot(low[lax.div(order_ref[i], depth)], adj_sorted[i])
            segs[i + 1] = part + keep_ref[i] * segs[i]
            return 0

        lax.fori_loop(0, slots, term, 0, unroll=4)

        def rim_tile(j):
            return segs[last_ref[j]].astype(BF16)

        def send(i, _):
            p = node_peer(i + 1)
            for s in range(2):
                rim_send[b, p, s] = rim_tile(blocks + 2 * p + s)
            pltpu.make_async_remote_copy(
                src_ref=rim_send.at[b, p], dst_ref=rim_recv.at[b, me_q],
                send_sem=r_ss.at[b], recv_sem=r_rs.at[b],
                device_id=(p, me_f), device_id_type=MESH,
            ).start()
            return 0

        lax.fori_loop(0, n_nodes - 1, send, 0)
        for s in range(2):
            rim_recv[b, me_q, s] = rim_tile(blocks + 2 * me_q + s)

        def local(t, _):
            gm[:, lanes(t, TILE)] = segs[last_ref[t]]
            return 0

        lax.fori_loop(0, blocks, local, 0)

    def rim_wait(b):
        here = rim_recv.at[b, pl.ds(0, n_nodes - 1)]
        pltpu.make_async_remote_copy(
            src_ref=here, dst_ref=here, send_sem=r_ss.at[b], recv_sem=r_rs.at[b],
            device_id=(node_peer(1), me_f), device_id_type=MESH,
        ).wait_recv()

    def scatter(b):
        def step(c, _):
            acc = gm[:, lanes(c)]
            for p in range(n_nodes):
                value = jnp.concatenate([rim_recv[b, p, 0], rim_recv[b, p, 1]], axis=1)
                acc = acc + dot(value, spread[p, :, lanes(c)])
            gm[:, lanes(c)] = acc
            gml[b, :, lanes(c)] = acc.astype(BF16)
            return 0

        lax.fori_loop(0, chunks, step, 0)

    def pull_back(b, layer, group, g):
        def step(c, _):
            gnorm = dot(weights_ref[layer, group], gml[b, :, lanes(c)]) * dgate[b, :, lanes(c)]
            norm = normed[b, :, lanes(c)]
            first = jnp.sum(gnorm, axis=0, keepdims=True) * (1.0 / total)
            second = jnp.sum(gnorm * norm, axis=0, keepdims=True) * (1.0 / total)
            g[:, lanes(c)] += inverse[b, :, lanes(c)] * (gnorm - first - norm * second)
            return 0

        lax.fori_loop(0, chunks, step, 0)

    def weight_send(b):
        mine = gm[pl.ds(pl.multiple_of(me_f * width, width), width), :].astype(BF16)
        part = dot_nt(mine, activ[b])
        gw_send[b] = part
        gw_recv[b, me_q] = part
        for d in range(1, n_nodes):
            pltpu.make_async_remote_copy(
                src_ref=gw_send.at[b], dst_ref=gw_recv.at[b, me_q],
                send_sem=w_ss.at[b], recv_sem=w_rs.at[b],
                device_id=(node_peer(d), me_f), device_id_type=MESH,
            ).start()

    def mine(ref):
        return ref[pl.ds(pl.multiple_of(me_f * width, width), width), :]

    take_gathered(0)
    activate(x2, 0, False)
    mix_and_send(0, 0, 0)
    take_gathered(1)
    gates(0)
    halo_wait(0)
    aggregate(0, x1)

    activate(x1, 1, False)
    mix_and_send(1, 0, 1)
    take_gathered(2)
    take_gathered(3)
    gates(1)
    rims_and_send(3, g2)
    halo_wait(1)
    aggregate(1, x2)

    activate(x2, 2, False)
    mix_and_send(2, 1, 0)
    gates(2)
    rim_wait(3)
    scatter(3)
    halo_wait(2)
    aggregate(2, x1)

    activate(x1, 3, True)
    out_ref[0] = mine(x1)
    pull_back(3, 1, 1, g1)
    weight_send(3)

    rims_and_send(2, g1)
    mix_and_send(3, 1, 1)
    rim_wait(2)
    scatter(2)
    pull_back(2, 1, 0, g2)
    weight_send(2)

    rims_and_send(1, g2)
    halo_wait(3)
    aggregate(3, x2)
    out_ref[1] = mine(x2)
    rim_wait(1)
    scatter(1)
    pull_back(1, 0, 1, g1)
    weight_send(1)

    rims_and_send(0, g1)
    sg_ref[0] = mine(g1)
    rim_wait(0)
    scatter(0)
    weight_send(0)
    pull_back(0, 0, 0, g2)
    sg_ref[1] = mine(g2)

    for b in range(4):
        here = gw_recv.at[b, pl.ds(0, n_nodes - 1)]
        pltpu.make_async_remote_copy(
            src_ref=here, dst_ref=here, send_sem=w_ss.at[b], recv_sem=w_rs.at[b],
            device_id=(node_peer(1), me_f), device_id_type=MESH,
        ).wait()
        summed = gw_recv[b, 0]
        for p in range(1, n_nodes):
            summed = summed + gw_recv[b, p]
        wg_ref[b // 2, b % 2] = summed
        here = src[b].at[pl.ds(blocks, 2 * (n_nodes - 1))]
        pltpu.make_async_remote_copy(
            src_ref=here, dst_ref=here, send_sem=h_ss.at[b], recv_sem=h_rs.at[b],
            device_id=(node_peer(1), me_f), device_id_type=MESH,
        ).wait_send()
        here = rim_recv.at[b, pl.ds(0, n_nodes - 1)]
        pltpu.make_async_remote_copy(
            src_ref=here, dst_ref=here, send_sem=r_ss.at[b], recv_sem=r_rs.at[b],
            device_id=(node_peer(1), me_f), device_id_type=MESH,
        ).wait_send()
        here = ag_recv.at[b, pl.ds(0, n_feat - 1)]
        pltpu.make_async_remote_copy(
            src_ref=here, dst_ref=here, send_sem=ag_ss.at[b], recv_sem=ag_rs.at[b],
            device_id=(me_q, feat_peer(1)), device_id_type=MESH,
        ).wait_send()


def sorted_slots(tile_source, source_tiles):
    source = tile_source.reshape(-1)
    n = source.shape[0]
    place = jnp.arange(n, dtype=jnp.int32)
    key = source * n + place
    rank = jnp.sum((key[None, :] < key[:, None]).astype(jnp.int32), axis=1)
    at = rank[None, :] == place[:, None]
    order = jnp.sum(jnp.where(at, place[None, :], 0), axis=1)
    ordered = jnp.sum(jnp.where(at, source[None, :], 0), axis=1)
    keep = jnp.concatenate([jnp.zeros((1,), F32), (ordered[1:] == ordered[:-1]).astype(F32)])
    tiles = jnp.arange(source_tiles, dtype=jnp.int32)
    upto = jnp.sum((source[None, :] <= tiles[:, None]).astype(jnp.int32), axis=1)
    has = jnp.any(source[None, :] == tiles[:, None], axis=1)
    return order, keep, jnp.where(has, upto, 0)


def solution(mesh):
    n_nodes, n_feat = mesh.shape["nodes"], mesh.shape["feat"]

    def body(node_states, weights, adj_tiles, tile_source, tile_count, send_rows, send_count, out_grads):
        groups, width, rows = node_states.shape
        total = width * n_feat
        blocks, depth = tile_source.shape
        slots = send_rows.shape[2]
        source_tiles = blocks + n_nodes * slots // TILE
        order, keep, last = sorted_slots(tile_source, source_tiles)
        vmem = pl.BlockSpec(memory_space=pltpu.VMEM)
        smem = pl.BlockSpec(memory_space=pltpu.SMEM)
        dma = pltpu.SemaphoreType.DMA((4,))
        outs = pl.pallas_call(
            functools.partial(kernel, n_nodes, n_feat),
            out_shape=(
                jax.ShapeDtypeStruct(node_states.shape, F32),
                jax.ShapeDtypeStruct(out_grads.shape, F32),
                jax.ShapeDtypeStruct((2, 2, width, total), F32),
            ),
            in_specs=[vmem] * 5 + [smem] * 6,
            out_specs=(vmem, vmem, vmem),
            scratch_shapes=[
                pltpu.VMEM((4, 2 * width, rows // 2), BF16),
                pltpu.VMEM((4, n_feat, 2 * width, rows // 2), BF16),
                pltpu.VMEM((total, rows), F32),
                pltpu.VMEM((total, rows), F32),
                pltpu.VMEM((total, rows), F32),
                pltpu.VMEM((total, rows), F32),
                pltpu.VMEM((2, 2, total, total), BF16),
                pltpu.VMEM((blocks, depth * TILE, TILE), BF16),
                pltpu.VMEM((blocks * depth, TILE, TILE), BF16),
                pltpu.VMEM((n_nodes, rows, slots), BF16),
                pltpu.VMEM((n_nodes, slots, rows), BF16),
                pltpu.VMEM((4, total, rows), F32),
                pltpu.VMEM((4, total, rows), F32),
                pltpu.VMEM((4, total, rows), BF16),
                pltpu.VMEM((4, 1, rows), F32),
                pltpu.VMEM((total, rows), BF16),
                *[pltpu.VMEM((source_tiles, total, TILE), BF16)] * 4,
                pltpu.VMEM((4, n_nodes, 2, total, TILE), BF16),
                pltpu.VMEM((blocks, total, TILE), BF16),
                pltpu.VMEM((blocks * depth + 1, total, TILE), F32),
                pltpu.VMEM((4, n_nodes, 2, total, TILE), BF16),
                pltpu.VMEM((4, n_nodes, 2, total, TILE), BF16),
                pltpu.VMEM((total, rows), F32),
                pltpu.VMEM((4, total, rows), BF16),
                pltpu.VMEM((4, width, total), F32),
                pltpu.VMEM((4, n_nodes, width, total), F32),
                dma, dma, dma, dma, dma, dma, dma, dma,
            ],
            compiler_params=pltpu.CompilerParams(
                collective_id=0, has_side_effects=True, vmem_limit_bytes=62 * 2**20
            ),
        )(
            node_states, out_grads, weights, adj_tiles, send_rows,
            tile_source, tile_count, send_count, order, keep, last,
        )
        return outs[0], outs[1], jnp.swapaxes(outs[2], 2, 3)

    return jax.shard_map(
        body,
        mesh=mesh,
        in_specs=(
            P(None, "feat", "nodes"),
            P(),
            P("nodes", None, None, None),
            P("nodes", None),
            P("nodes"),
            P("nodes", None, None),
            P("nodes", None),
            P(None, "feat", "nodes"),
        ),
        out_specs=(P(None, "feat", "nodes"), P(None, "feat", "nodes"), P(None, None, None, "feat")),
        check_vma=False,
    )
```

```python
import functools

import jax
import jax.numpy as jnp
from jax import lax
from jax.experimental import pallas as pl
from jax.experimental.pallas import tpu as pltpu
from jax.sharding import PartitionSpec as P

MESH = pl.DeviceIdType.MESH
TILE = 128
EPS = 1e-05
TERM_UNROLL = 8
F32 = jnp.float32
BF16 = jnp.bfloat16


def dot(a, b):
    return jnp.dot(a, b, preferred_element_type=F32)


def dot_nt(a, b):
    return lax.dot_general(a, b, (((1,), (1,)), ((), ())), preferred_element_type=F32)


def kernel(
    n_nodes, n_feat,
    states_ref, grads_ref, weights_ref, adj_hbm, rows_ref,
    source_ref, count_ref, sent_ref,
    out_ref, sg_ref, wg_ref,
    adj_ref, plan_rows, plan, local_sems,
    ag_send, ag_recv, x1, x2, g1, g2, wt,
    fwd_tiles, adj_sorted, pick, spread,
    normed, dgate, activ, inverse, mixed,
    src0, src1, src2, src3, halo_out, low, segs, rim_out, rim_in, gm, gml,
    gw_send, gw_recv,
    ag_ss, ag_rs, h_ss, h_rs, r_ss, r_rs, w_ss, w_rs,
):
    src = (src0, src1, src2, src3)
    me_q = lax.axis_index("nodes")
    me_f = lax.axis_index("feat")
    width = states_ref.shape[1]
    rows = states_ref.shape[2]
    total = width * n_feat
    half = rows // 2
    blocks = rows // TILE
    chunks = rows // 256
    depth = adj_ref.shape[1]
    slots = blocks * depth
    adj_copy = pltpu.make_async_copy(adj_hbm, adj_ref, local_sems.at[0])
    adj_copy.start()

    me_x, me_c = lax.div(me_q, 2), lax.rem(me_q, 2)
    me_z, me_y = lax.div(me_f, 4), lax.rem(me_f, 4)

    def node_peer(shift):
        dx, dc = shift
        return lax.rem(me_x + dx, n_nodes // 2) * 2 + lax.rem(me_c + dc, 2)

    def feat_peer(shift):
        dz, dy = shift
        return lax.rem(me_z + dz, n_feat // 4) * 4 + lax.rem(me_y + dy, 4)

    def hops(shift):
        return min(shift[0], 4 - shift[0]) + min(shift[1], 4 - shift[1])

    feat_shifts = [(dz, dy) for dz in range(4) for dy in range(4) if dz or dy]
    feat_shifts.sort(key=lambda shift: -hops(shift))
    mate = (0, 1)
    groups = [((2, 0), (2, 1)), ((1, 0), (3, 0)), ((1, 1), (3, 1))]
    far_shifts = [shift for group in groups for shift in group]
    node_shifts = far_shifts + [mate]

    def back(shift):
        return ((4 - shift[0]) % 4, shift[1])

    started = []
    barrier = pltpu.get_barrier_semaphore()
    for shift in feat_shifts:
        pl.semaphore_signal(barrier, inc=1, device_id=(me_q, feat_peer(shift)), device_id_type=MESH)
    for shift in node_shifts:
        pl.semaphore_signal(barrier, inc=1, device_id=(node_peer(shift), me_f), device_id_type=MESH)

    gathered = [(states_ref, 1, x2), (states_ref, 0, x1), (grads_ref, 1, g2), (grads_ref, 0, g1)]
    for a, (ref, group, _) in enumerate(gathered):
        packed = jnp.concatenate([ref[group, :, :half], ref[group, :, half:]], axis=0).astype(BF16)
        ag_send[a] = packed
        ag_recv[a, me_f] = packed
    for layer in range(2):
        for group in range(2):
            wt[layer, group] = weights_ref[layer, group].astype(F32).T.astype(BF16)

    lane = lax.broadcasted_iota(jnp.int32, (1, TILE), 1)
    source = jnp.full((1, TILE), blocks * TILE, jnp.int32)
    for e in range(slots):
        source = jnp.where(lane == e, source_ref[e // blocks, e % blocks], source)
    place = lax.broadcasted_iota(jnp.int32, (TILE, TILE), 0)
    lanes_of = lax.broadcasted_iota(jnp.int32, (TILE, TILE), 1)

    def column(row):
        return jnp.broadcast_to(row, (TILE, TILE)).T

    source_column = column(source)
    key = source * TILE + lane
    rank = column(jnp.sum((column(key) < key).astype(jnp.int32), axis=0, keepdims=True))
    at = rank == lanes_of
    before = rank + 1 == lanes_of
    order = jnp.sum(jnp.where(at, place, 0), axis=0, keepdims=True)
    ordered = jnp.sum(jnp.where(at, source_column, 0), axis=0, keepdims=True)
    previous = jnp.sum(jnp.where(before, source_column, 0), axis=0, keepdims=True)
    keep = jnp.where((ordered == previous) & (lane > 0), 1, 0)
    upto = jnp.sum((source_column <= lanes_of).astype(jnp.int32), axis=0, keepdims=True)
    has = jnp.sum((source_column == lanes_of).astype(jnp.int32), axis=0, keepdims=True)
    plan_rows[0:1, :] = order
    plan_rows[1:2, :] = keep
    plan_rows[2:3, :] = jnp.where(has > 0, upto, 0)
    plan_copy = pltpu.make_async_copy(plan_rows, plan, local_sems.at[1])
    plan_copy.start()

    def prepare_block(t, _):
        for k in range(depth):
            keep = (k < count_ref[t]).astype(F32)
            tile = adj_ref[t, k].astype(F32) * keep
            fwd_tiles[t, k * TILE:(k + 1) * TILE, :] = tile.T.astype(BF16)
        return 0

    adj_copy.wait()
    lax.fori_loop(0, blocks, prepare_block, 0)

    def prepare_sorted(i, _):
        e = plan[0, i]
        t = lax.rem(e, blocks)
        k = lax.div(e, blocks)
        keep = (k < count_ref[t]).astype(F32)
        adj_sorted[i] = (adj_ref[t, k].astype(F32) * keep).astype(BF16)
        return 0

    plan_copy.wait()
    lax.fori_loop(0, slots, prepare_sorted, 0)

    def prepare_pick(p, _):
        lane = lax.broadcasted_iota(jnp.int32, (1, 256), 1)
        index = jnp.where(lane < sent_ref[0, p], rows_ref[0, pl.ds(p, 1), :], -1)
        high = lax.broadcasted_iota(jnp.int32, (256, 256), 0)
        for c in range(chunks):
            hit = high + c * 256 == index
            pick[p, c * 256:(c + 1) * 256, :] = jnp.where(hit, 1.0, 0.0).astype(BF16)
        value = index.astype(F32)
        place = lax.broadcasted_iota(jnp.int32, (TILE, 256), 1).astype(F32)
        for s in range(2):
            column = jnp.broadcast_to(value[:, s * TILE:(s + 1) * TILE], (TILE, TILE)).T
            column = jnp.concatenate([column, column], axis=1)
            for c in range(chunks):
                hit = place + float(c * 256) == column
                spread[p, s * TILE:(s + 1) * TILE, c * 256:(c + 1) * 256] = jnp.where(hit, 1.0, 0.0).astype(BF16)
        return 0

    lax.fori_loop(0, n_nodes, prepare_pick, 0)

    pl.semaphore_wait(barrier, n_feat - 1 + n_nodes - 1)

    def send_gathered(a):
        for shift in feat_shifts:
            pltpu.make_async_remote_copy(
                src_ref=ag_send.at[a], dst_ref=ag_recv.at[a, me_f],
                send_sem=ag_ss.at[a], recv_sem=ag_rs.at[a],
                device_id=(me_q, feat_peer(shift)), device_id_type=MESH,
            ).start()

    send_gathered(0)
    send_gathered(1)

    def take_gathered(a):
        ref, group, target = gathered[a]
        pltpu.make_async_remote_copy(
            src_ref=ag_recv.at[a, pl.ds(0, n_feat - 1)], dst_ref=ag_recv.at[a, pl.ds(0, n_feat - 1)],
            send_sem=ag_ss.at[a], recv_sem=ag_rs.at[a],
            device_id=(me_q, feat_peer((0, 1))), device_id_type=MESH,
        ).wait_recv()
        for f in range(n_feat):
            got = ag_recv[a, f].astype(F32)
            target[f * width:(f + 1) * width, :half] = got[:width]
            target[f * width:(f + 1) * width, half:] = got[width:]
        target[pl.ds(pl.multiple_of(me_f * width, width), width), :] = ref[group]

    def lanes(c, size=256):
        return pl.ds(pl.multiple_of(c * size, size), size)

    def copy_to_node(source, target, sends, receives, shift):
        return pltpu.make_async_remote_copy(
            src_ref=source, dst_ref=target, send_sem=sends, recv_sem=receives,
            device_id=(node_peer(shift), me_f), device_id_type=MESH,
        )

    def forward(b, layer, group, u, add=None, with_gate=False):
        def step(c, _):
            states = u[:, lanes(c)]
            if add is not None:
                parts = []
                for h in range(2):
                    tiles = [src[add][source_ref[k, 2 * c + h]] for k in range(depth)]
                    parts.append(dot(jnp.concatenate(tiles, axis=1), fwd_tiles[2 * c + h]))
                states = states + jnp.concatenate(parts, axis=1)
                u[:, lanes(c)] = states
            center = jnp.sum(states, axis=0, keepdims=True) * (1.0 / total)
            square = jnp.sum(states * states, axis=0, keepdims=True) * (1.0 / total)
            inv = lax.rsqrt(square - center * center + EPS)
            norm = (states - center) * inv
            gate = 1.0 / (1.0 + jnp.exp(-norm))
            normed[b, :, lanes(c)] = norm
            inverse[b, :, lanes(c)] = inv
            act = (norm * gate).astype(BF16)
            activ[b, :, lanes(c)] = act
            if with_gate:
                dgate[b, :, lanes(c)] = gate * (1.0 + norm * (1.0 - gate))
            value = dot(wt[layer, group], act).astype(BF16)
            mixed[:, lanes(c)] = value
            src[b][2 * c] = value[:, :TILE]
            src[b][2 * c + 1] = value[:, TILE:]
            return 0

        lax.fori_loop(0, chunks, step, 0, unroll=2)

    def aggregate(b, u):
        def step(t, _):
            tiles = [src[b][source_ref[k, t]] for k in range(depth)]
            u[:, lanes(t, TILE)] += dot(jnp.concatenate(tiles, axis=1), fwd_tiles[t])
            return 0

        lax.fori_loop(0, blocks, step, 0, unroll=4)

    def gates(b):
        def step(c, _):
            norm = normed[b, :, lanes(c)]
            gate = 1.0 / (1.0 + jnp.exp(-norm))
            dgate[b, :, lanes(c)] = gate * (1.0 + norm * (1.0 - gate))
            return 0

        lax.fori_loop(0, chunks, step, 0)

    def halo_send(b):
        for shift in node_shifts:
            p = node_peer(shift)
            value = dot(mixed[...], pick[p]).astype(BF16)
            halo_out[b, p, 0] = value[:, :TILE]
            halo_out[b, p, 1] = value[:, TILE:]
            copy_to_node(
                halo_out.at[b, p], src[b].at[pl.ds(blocks + 2 * me_q, 2)], h_ss.at[b], h_rs.at[b], shift
            ).start()
        started.append((h_ss.at[b], src[b].at[pl.ds(blocks, 2 * (n_nodes - 1))]))
        value = dot(mixed[...], pick[me_q]).astype(BF16)
        src[b][blocks + 2 * me_q] = value[:, :TILE]
        src[b][blocks + 2 * me_q + 1] = value[:, TILE:]

    def halo_wait(b):
        here = src[b].at[pl.ds(blocks, 2 * (n_nodes - 1))]
        copy_to_node(here, here, h_ss.at[b], h_rs.at[b], mate).wait_recv()

    def lower(g):
        def step(t, _):
            low[t] = g[:, lanes(t, TILE)].astype(BF16)
            return 0

        lax.fori_loop(0, blocks, step, 0)

    def terms():
        segs[0] = jnp.zeros((total, TILE), F32)

        def step(j, _):
            acc = segs[TERM_UNROLL * j]
            for n in range(TERM_UNROLL):
                i = TERM_UNROLL * j + n
                part = dot(low[lax.rem(plan[0, i], blocks)], adj_sorted[i])
                acc = part + plan[1, i].astype(F32) * acc
                segs[i + 1] = acc
            return 0

        lax.fori_loop(0, slots // TERM_UNROLL, step, 0)

    def rim_send(b):
        def rim(p):
            tiles = [segs[plan[2, blocks + 2 * p + s]] for s in range(2)]
            return jnp.concatenate(tiles, axis=1).astype(BF16)

        for n, shift in enumerate([mate] + far_shifts):
            p = node_peer(shift)
            rim_out[b, p] = rim(p)
            copy_to_node(
                rim_out.at[b, p], rim_in.at[b, me_q], r_ss.at[b], r_rs.at[b, (n + 1) // 2], shift
            ).start()
        started.append((r_ss.at[b], rim_in.at[b, pl.ds(0, n_nodes - 1)]))
        own = rim(me_q)

        def local(c, _):
            tiles = [segs[plan[2, 2 * c + h]] for h in range(2)]
            gm[:, lanes(c)] = jnp.concatenate(tiles, axis=1) + dot(own, spread[me_q, :, lanes(c)])
            return 0

        lax.fori_loop(0, chunks, local, 0, unroll=2)

    def rim_wait(b, n):
        here = rim_in.at[b, pl.ds(0, 1 if n == 0 else 2)]
        copy_to_node(here, here, r_ss.at[b], r_rs.at[b, n], mate).wait_recv()

    def rim_add(b, n):
        rim_wait(b, n)
        peers = [node_peer(back(shift)) for shift in ([mate] if n == 0 else groups[n - 1])]

        def step(c, _):
            acc = gm[:, lanes(c)]
            for p in peers:
                acc = acc + dot(rim_in[b, p], spread[p, :, lanes(c)])
            gm[:, lanes(c)] = acc
            return 0

        lax.fori_loop(0, chunks, step, 0, unroll=2)

    def pull_back(b, layer, group, g, last=True):
        if last:
            rim_wait(b, 3)
            peers = [node_peer(back(shift)) for shift in groups[2]]

        def step(c, _):
            acc = gm[:, lanes(c)]
            if last:
                for p in peers:
                    acc = acc + dot(rim_in[b, p], spread[p, :, lanes(c)])
            value = acc.astype(BF16)
            gml[:, lanes(c)] = value
            gnorm = dot(weights_ref[layer, group], value) * dgate[b, :, lanes(c)]
            norm = normed[b, :, lanes(c)]
            first = jnp.sum(gnorm, axis=0, keepdims=True) * (1.0 / total)
            second = jnp.sum(gnorm * norm, axis=0, keepdims=True) * (1.0 / total)
            state = g[:, lanes(c)] + inverse[b, :, lanes(c)] * (gnorm - first - norm * second)
            g[:, lanes(c)] = state
            state = state.astype(BF16)
            low[2 * c] = state[:, :TILE]
            low[2 * c + 1] = state[:, TILE:]
            return 0

        lax.fori_loop(0, chunks, step, 0, unroll=2)

    def weight_send(b):
        own = gml[pl.ds(pl.multiple_of(lax.div(me_f, 2) * 2 * width, 2 * width), 2 * width), :]
        part = dot_nt(own, activ[b])
        part = jnp.where(lax.rem(me_f, 2) == 0, part[:width], part[width:])
        gw_send[b] = part
        gw_recv[b, me_q] = part
        for shift in node_shifts:
            copy_to_node(gw_send.at[b], gw_recv.at[b, me_q], w_ss.at[b], w_rs.at[b], shift).start()

    def mine(ref):
        return ref[pl.ds(pl.multiple_of(me_f * width, width), width), :]

    take_gathered(0)
    forward(0, 0, 0, x2)
    halo_send(0)
    send_gathered(2)
    take_gathered(1)
    gates(0)
    halo_wait(0)

    forward(1, 0, 1, x1, add=0)
    halo_send(1)
    send_gathered(3)
    gates(1)
    take_gathered(2)
    lower(g2)
    terms()
    rim_send(3)
    halo_wait(1)

    forward(2, 1, 0, x2, add=1)
    halo_send(2)
    gates(2)
    take_gathered(3)
    rim_add(3, 0)
    rim_add(3, 1)
    rim_add(3, 2)
    rim_add(3, 3)
    halo_wait(2)

    forward(3, 1, 1, x1, add=2, with_gate=True)
    pull_back(3, 1, 1, g1, last=False)
    terms()
    rim_send(2)
    weight_send(3)
    halo_send(3)
    out_ref[0] = mine(x1)
    rim_add(2, 0)
    rim_add(2, 1)
    rim_add(2, 2)
    pull_back(2, 1, 0, g2)

    terms()
    rim_send(1)
    weight_send(2)
    halo_wait(3)
    aggregate(3, x2)
    out_ref[1] = mine(x2)
    rim_add(1, 0)
    rim_add(1, 1)
    rim_add(1, 2)
    pull_back(1, 0, 1, g1)

    terms()
    rim_send(0)
    weight_send(1)
    sg_ref[0] = mine(g1)
    rim_add(0, 0)
    rim_add(0, 1)
    rim_add(0, 2)
    pull_back(0, 0, 0, g2)
    weight_send(0)
    sg_ref[1] = mine(g2)

    for b in range(4):
        here = gw_recv.at[b, pl.ds(0, n_nodes - 1)]
        pltpu.make_async_remote_copy(
            src_ref=here, dst_ref=here, send_sem=w_ss.at[b], recv_sem=w_rs.at[b],
            device_id=(node_peer(mate), me_f), device_id_type=MESH,
        ).wait()
        summed = gw_recv[b, 0]
        for p in range(1, n_nodes):
            summed = summed + gw_recv[b, p]
        wg_ref[b // 2, b % 2] = summed
        here = ag_recv.at[b, pl.ds(0, n_feat - 1)]
        pltpu.make_async_remote_copy(
            src_ref=here, dst_ref=here, send_sem=ag_ss.at[b], recv_sem=ag_rs.at[b],
            device_id=(me_q, feat_peer((0, 1))), device_id_type=MESH,
        ).wait_send()
    for sends, here in started:
        copy_to_node(here, here, sends, h_rs.at[0], mate).wait_send()


def hand_over(out, sg, wg, out_ref, sg_ref, wg_ref):
    out_ref[...] = out[...]
    sg_ref[...] = sg[...]
    wg_ref[...] = wg[...]


def solution(mesh):
    n_nodes, n_feat = mesh.shape["nodes"], mesh.shape["feat"]

    def body(node_states, weights, adj_tiles, tile_source, tile_count, send_rows, send_count, out_grads):
        groups, width, rows = node_states.shape
        total = width * n_feat
        blocks, depth = tile_source.shape
        slots = send_rows.shape[2]
        source_tiles = blocks + n_nodes * slots // TILE
        vmem = pl.BlockSpec(memory_space=pltpu.VMEM)
        smem = pl.BlockSpec(memory_space=pltpu.SMEM)
        dma = pltpu.SemaphoreType.DMA((4,))
        outs = pl.pallas_call(
            functools.partial(kernel, n_nodes, n_feat),
            out_shape=(
                jax.ShapeDtypeStruct(node_states.shape, F32),
                jax.ShapeDtypeStruct(out_grads.shape, F32),
                jax.ShapeDtypeStruct((2, 2, width, total), F32),
            ),
            in_specs=[vmem, vmem, vmem, pl.BlockSpec(memory_space=pl.ANY), vmem, smem, smem, smem],
            out_specs=(vmem, vmem, vmem),
            scratch_shapes=[
                pltpu.VMEM(adj_tiles.shape, BF16),
                pltpu.VMEM((8, TILE), jnp.int32),
                pltpu.SMEM((8, TILE), jnp.int32),
                pltpu.SemaphoreType.DMA((2,)),
                pltpu.VMEM((4, 2 * width, rows // 2), BF16),
                pltpu.VMEM((4, n_feat, 2 * width, rows // 2), BF16),
                pltpu.VMEM((total, rows), F32),
                pltpu.VMEM((total, rows), F32),
                pltpu.VMEM((total, rows), F32),
                pltpu.VMEM((total, rows), F32),
                pltpu.VMEM((2, 2, total, total), BF16),
                pltpu.VMEM((blocks, depth * TILE, TILE), BF16),
                pltpu.VMEM((blocks * depth, TILE, TILE), BF16),
                pltpu.VMEM((n_nodes, rows, slots), BF16),
                pltpu.VMEM((n_nodes, slots, rows), BF16),
                pltpu.VMEM((4, total, rows), F32),
                pltpu.VMEM((4, total, rows), F32),
                pltpu.VMEM((4, total, rows), BF16),
                pltpu.VMEM((4, 1, rows), F32),
                pltpu.VMEM((total, rows), BF16),
                *[pltpu.VMEM((source_tiles, total, TILE), BF16)] * 4,
                pltpu.VMEM((4, n_nodes, 2, total, TILE), BF16),
                pltpu.VMEM((blocks, total, TILE), BF16),
                pltpu.VMEM((blocks * depth + 1, total, TILE), F32),
                pltpu.VMEM((4, n_nodes, total, slots), BF16),
                pltpu.VMEM((4, n_nodes, total, slots), BF16),
                pltpu.VMEM((total, rows), F32),
                pltpu.VMEM((total, rows), BF16),
                pltpu.VMEM((4, width, total), F32),
                pltpu.VMEM((4, n_nodes, width, total), F32),
                dma, dma, dma, dma, dma, pltpu.SemaphoreType.DMA((4, 4)), dma, dma,
            ],
            compiler_params=pltpu.CompilerParams(
                collective_id=0, has_side_effects=True, vmem_limit_bytes=62 * 2**20
            ),
        )(
            node_states, out_grads, weights, adj_tiles, send_rows,
            tile_source.T, tile_count, send_count,
        )
        outs = pl.pallas_call(
            hand_over,
            out_shape=tuple(jax.ShapeDtypeStruct(o.shape, o.dtype) for o in outs),
            in_specs=[vmem] * 3,
            out_specs=(vmem,) * 3,
        )(*outs)
        return outs[0], outs[1], jnp.swapaxes(outs[2], 2, 3)

    return jax.shard_map(
        body,
        mesh=mesh,
        in_specs=(
            P(None, "feat", "nodes"),
            P(),
            P("nodes", None, None, None),
            P("nodes", None),
            P("nodes"),
            P("nodes", None, None),
            P("nodes", None),
            P(None, "feat", "nodes"),
        ),
        out_specs=(P(None, "feat", "nodes"), P(None, "feat", "nodes"), P(None, None, None, "feat")),
        check_vma=False,
    )
```

```python
import functools

import jax
import jax.numpy as jnp
from jax import lax
from jax.experimental import pallas as pl
from jax.experimental.pallas import tpu as pltpu
from jax.sharding import PartitionSpec as P

MESH = pl.DeviceIdType.MESH
TILE = 128
EPS = 1e-05
TERM_UNROLL = 8
F32 = jnp.float32
BF16 = jnp.bfloat16


def dot(a, b):
    return jnp.dot(a, b, preferred_element_type=F32)


def dot_nt(a, b):
    return lax.dot_general(a, b, (((1,), (1,)), ((), ())), preferred_element_type=F32)


def kernel(
    n_nodes, n_feat,
    states_hbm, grads_hbm, weights_hbm, adj_hbm, rows_hbm,
    source_ref, count_ref, sent_ref,
    out_hbm, sg_hbm, wg_hbm,
    states_ref, grads_ref, weights_ref, rows_ref, out_ref, sg_ref, wg_ref,
    adj_ref, plan_rows, plan, local_sems,
    ag_send, ag_recv, line_send, line_recv, line_ss, line_rs, x1, x2, g1, g2, wt,
    fwd_tiles, adj_sorted, pick, spread,
    normed, dgate, activ, inverse, mixed,
    src0, src1, src2, src3, halo_out, low, segs, rim_out, rim_in, gm, gml,
    gw_send, gw_recv, own_in, gml16, out_sems,
    ag_ss, ag_rs, h_ss, h_rs, r_ss, r_rs, w_ss, w_rs, own_sems,
):
    src = (src0, src1, src2, src3)
    me_q = lax.axis_index("nodes")
    me_f = lax.axis_index("feat")
    width = states_ref.shape[1]
    rows = states_ref.shape[2]
    total = width * n_feat
    half = rows // 2
    blocks = rows // TILE
    chunks = rows // 256
    depth = adj_ref.shape[1]
    slots = blocks * depth

    me_x, me_c = lax.div(me_q, 2), lax.rem(me_q, 2)
    me_z, me_y = lax.div(me_f, 4), lax.rem(me_f, 4)

    def node_peer(shift):
        dx, dc = shift
        return lax.rem(me_x + dx, n_nodes // 2) * 2 + lax.rem(me_c + dc, 2)

    def feat_peer(shift):
        dz, dy = shift
        return lax.rem(me_z + dz, n_feat // 4) * 4 + lax.rem(me_y + dy, 4)

    def hops(shift):
        return min(shift[0], 4 - shift[0]) + min(shift[1], 4 - shift[1])

    feat_shifts = [(dz, dy) for dz in range(4) for dy in range(4) if dz or dy]
    feat_shifts.sort(key=lambda shift: -hops(shift))
    mate = (0, 1)
    groups = [((2, 0), (2, 1)), ((1, 0), (3, 0)), ((1, 1), (3, 1))]
    far_shifts = [shift for group in groups for shift in group]
    node_shifts = far_shifts + [mate]

    def back(shift):
        return ((4 - shift[0]) % 4, shift[1])

    started = []
    started_feat = []
    barrier = pltpu.get_barrier_semaphore()
    for shift in feat_shifts:
        pl.semaphore_signal(barrier, inc=1, device_id=(me_q, feat_peer(shift)), device_id_type=MESH)
    for shift in node_shifts:
        pl.semaphore_signal(barrier, inc=1, device_id=(node_peer(shift), me_f), device_id_type=MESH)

    states_copy = pltpu.make_async_copy(states_hbm, states_ref, local_sems.at[2])
    grads_copy = pltpu.make_async_copy(grads_hbm, grads_ref, local_sems.at[3])
    rows_copy = pltpu.make_async_copy(rows_hbm, rows_ref, local_sems.at[4])
    weights_copy = pltpu.make_async_copy(weights_hbm, weights_ref, local_sems.at[5])
    adj_copy = pltpu.make_async_copy(adj_hbm, adj_ref, local_sems.at[0])
    for copy in (states_copy, grads_copy, rows_copy, weights_copy, adj_copy):
        copy.start()
    states_copy.wait()
    grads_copy.wait()

    gathered = [(states_ref, 1, x2), (states_ref, 0, x1), (grads_ref, 1, g2), (grads_ref, 0, g1)]
    for a, (ref, group, _) in enumerate(gathered):
        packed = jnp.concatenate([ref[group, :, :half], ref[group, :, half:]], axis=0).astype(BF16)
        if a == 0:
            ag_send[...] = packed
            ag_recv[me_f] = packed
        else:
            quarter = half // 2
            line_send[a - 1, 0] = packed[:, :quarter]
            line_send[a - 1, 1] = packed[:, quarter:]
            line_recv[a - 1, 0, me_z, me_y] = packed[:, :quarter]
            line_recv[a - 1, 1, me_y, me_z] = packed[:, quarter:]
    weights_copy.wait()
    for layer in range(2):
        for group in range(2):
            wt[layer, group] = weights_ref[layer, group].astype(F32).T.astype(BF16)

    lane = lax.broadcasted_iota(jnp.int32, (1, TILE), 1)
    source = jnp.full((1, TILE), blocks * TILE, jnp.int32)
    for e in range(slots):
        source = jnp.where(lane == e, source_ref[e // blocks, e % blocks], source)
    place = lax.broadcasted_iota(jnp.int32, (TILE, TILE), 0)
    lanes_of = lax.broadcasted_iota(jnp.int32, (TILE, TILE), 1)

    def column(row):
        return jnp.broadcast_to(row, (TILE, TILE)).T

    source_column = column(source)
    key = source * TILE + lane
    rank = column(jnp.sum((column(key) < key).astype(jnp.int32), axis=0, keepdims=True))
    at = rank == lanes_of
    before = rank + 1 == lanes_of
    order = jnp.sum(jnp.where(at, place, 0), axis=0, keepdims=True)
    ordered = jnp.sum(jnp.where(at, source_column, 0), axis=0, keepdims=True)
    previous = jnp.sum(jnp.where(before, source_column, 0), axis=0, keepdims=True)
    keep = jnp.where((ordered == previous) & (lane > 0), 1, 0)
    upto = jnp.sum((source_column <= lanes_of).astype(jnp.int32), axis=0, keepdims=True)
    has = jnp.sum((source_column == lanes_of).astype(jnp.int32), axis=0, keepdims=True)
    plan_rows[0:1, :] = order
    plan_rows[1:2, :] = keep
    plan_rows[2:3, :] = jnp.where(has > 0, upto, 0)
    plan_copy = pltpu.make_async_copy(plan_rows, plan, local_sems.at[1])
    plan_copy.start()

    def prepare_block(t, _):
        for k in range(depth):
            keep = (k < count_ref[t]).astype(F32)
            tile = adj_ref[t, k].astype(F32) * keep
            fwd_tiles[t, k * TILE:(k + 1) * TILE, :] = tile.T.astype(BF16)
        return 0

    adj_copy.wait()
    lax.fori_loop(0, blocks, prepare_block, 0)

    def prepare_sorted(i, _):
        e = plan[0, i]
        t = lax.rem(e, blocks)
        k = lax.div(e, blocks)
        keep = (k < count_ref[t]).astype(F32)
        adj_sorted[i] = (adj_ref[t, k].astype(F32) * keep).astype(BF16)
        return 0

    plan_copy.wait()
    lax.fori_loop(0, slots, prepare_sorted, 0)

    def prepare_pick(p, _):
        lane = lax.broadcasted_iota(jnp.int32, (1, 256), 1)
        index = jnp.where(lane < sent_ref[0, p], rows_ref[0, pl.ds(p, 1), :], -1)
        high = lax.broadcasted_iota(jnp.int32, (256, 256), 0)
        for c in range(chunks):
            hit = high + c * 256 == index
            pick[p, c * 256:(c + 1) * 256, :] = jnp.where(hit, 1.0, 0.0).astype(BF16)
        value = index.astype(F32)
        place = lax.broadcasted_iota(jnp.int32, (TILE, 256), 1).astype(F32)
        for s in range(2):
            column = jnp.broadcast_to(value[:, s * TILE:(s + 1) * TILE], (TILE, TILE)).T
            column = jnp.concatenate([column, column], axis=1)
            for c in range(chunks):
                hit = place + float(c * 256) == column
                spread[p, s * TILE:(s + 1) * TILE, c * 256:(c + 1) * 256] = jnp.where(hit, 1.0, 0.0).astype(BF16)
        return 0

    rows_copy.wait()
    lax.fori_loop(0, n_nodes, prepare_pick, 0)

    pl.semaphore_wait(barrier, n_feat - 1 + n_nodes - 1)

    def copy_to_feat(source, target, sends, receives, shift):
        return pltpu.make_async_remote_copy(
            src_ref=source, dst_ref=target, send_sem=sends, recv_sem=receives,
            device_id=(me_q, feat_peer(shift)), device_id_type=MESH,
        )

    lines = ([(0, 2), (0, 1), (0, 3)], [(2, 0), (1, 0), (3, 0)])
    place_of = ((me_z, me_y), (me_y, me_z))

    def send_direct():
        for shift in feat_shifts:
            copy_to_feat(ag_send, ag_recv.at[me_f], ag_ss.at[0], ag_rs.at[0], shift).start()
        started_feat.append((ag_ss.at[0], ag_recv.at[pl.ds(0, n_feat - 1)]))

    def send_lines(a):
        for w in range(2):
            first, second = place_of[w]
            for shift in lines[w]:
                copy_to_feat(
                    line_send.at[a - 1, w], line_recv.at[a - 1, w, first, second],
                    line_ss.at[a, w], line_rs.at[a, w], shift,
                ).start()
            started_feat.append((line_ss.at[a, w], line_recv.at[a - 1, w, 0, pl.ds(0, 3)]))

    def relay_lines(a):
        for w in range(2):
            here = line_recv.at[a - 1, w, 0, pl.ds(0, 3)]
            copy_to_feat(here, here, line_ss.at[a, w], line_rs.at[a, w], (0, 1)).wait_recv()
            first = place_of[w][0]
            for shift in lines[1 - w]:
                copy_to_feat(
                    line_recv.at[a - 1, w, first], line_recv.at[a - 1, w, first],
                    line_ss.at[a, 2 + w], line_rs.at[a, 2 + w], shift,
                ).start()
            started_feat.append((line_ss.at[a, 2 + w], line_recv.at[a - 1, w, pl.ds(0, 3)]))

    send_direct()
    for a in range(1, 4):
        send_lines(a)

    def take_gathered(a):
        ref, group, target = gathered[a]
        if a == 0:
            here = ag_recv.at[pl.ds(0, n_feat - 1)]
            copy_to_feat(here, here, ag_ss.at[0], ag_rs.at[0], (0, 1)).wait_recv()
            for f in range(n_feat):
                got = ag_recv[f].astype(F32)
                target[f * width:(f + 1) * width, :half] = got[:width]
                target[f * width:(f + 1) * width, half:] = got[width:]
        else:
            quarter = half // 2
            for w in range(2):
                here = line_recv.at[a - 1, w, pl.ds(0, 3)]
                copy_to_feat(here, here, line_ss.at[a, 2 + w], line_rs.at[a, 2 + w], (0, 1)).wait_recv()
                for f in range(n_feat):
                    z, y = f // 4, f % 4
                    got = line_recv[a - 1, w, (z, y)[w], (y, z)[w]].astype(F32)
                    at = w * quarter
                    target[f * width:(f + 1) * width, at:at + quarter] = got[:width]
                    target[f * width:(f + 1) * width, half + at:half + at + quarter] = got[width:]
        target[pl.ds(pl.multiple_of(me_f * width, width), width), :] = ref[group]

    def lanes(c, size=256):
        return pl.ds(pl.multiple_of(c * size, size), size)

    def copy_to_node(source, target, sends, receives, shift):
        return pltpu.make_async_remote_copy(
            src_ref=source, dst_ref=target, send_sem=sends, recv_sem=receives,
            device_id=(node_peer(shift), me_f), device_id_type=MESH,
        )

    def forward(b, layer, group, u, with_gate=False):
        def step(c, _):
            states = u[:, lanes(c)]
            center = jnp.sum(states, axis=0, keepdims=True) * (1.0 / total)
            square = jnp.sum(states * states, axis=0, keepdims=True) * (1.0 / total)
            inv = lax.rsqrt(square - center * center + EPS)
            norm = (states - center) * inv
            gate = 1.0 / (1.0 + jnp.exp(-norm))
            normed[b, :, lanes(c)] = norm
            inverse[b, :, lanes(c)] = inv
            act = (norm * gate).astype(BF16)
            activ[b, :, lanes(c)] = act
            if with_gate:
                dgate[b, :, lanes(c)] = gate * (1.0 + norm * (1.0 - gate))
            value = dot(wt[layer, group], act).astype(BF16)
            mixed[:, lanes(c)] = value
            src[b][2 * c] = value[:, :TILE]
            src[b][2 * c + 1] = value[:, TILE:]
            return 0

        lax.fori_loop(0, chunks, step, 0, unroll=2)

    def aggregate(b, u):
        def step(t, _):
            tiles = [src[b][source_ref[k, t]] for k in range(depth)]
            u[:, lanes(t, TILE)] += dot(jnp.concatenate(tiles, axis=1), fwd_tiles[t])
            return 0

        lax.fori_loop(0, blocks, step, 0, unroll=4)

    def gates(b):
        def step(c, _):
            norm = normed[b, :, lanes(c)]
            gate = 1.0 / (1.0 + jnp.exp(-norm))
            dgate[b, :, lanes(c)] = gate * (1.0 + norm * (1.0 - gate))
            return 0

        lax.fori_loop(0, chunks, step, 0)

    def halo_send(b):
        for n, shift in enumerate(node_shifts):
            p = node_peer(shift)
            value = dot(mixed[...], pick[p]).astype(BF16)
            halo_out[b, p, 0] = value[:, :TILE]
            halo_out[b, p, 1] = value[:, TILE:]
            copy_to_node(
                halo_out.at[b, p], src[b].at[pl.ds(blocks + 2 * me_q, 2)], h_ss.at[b], h_rs.at[b, n // 2], shift
            ).start()
        started.append((h_ss.at[b], src[b].at[pl.ds(blocks, 2 * (n_nodes - 1))]))
        value = dot(mixed[...], pick[me_q]).astype(BF16)
        src[b][blocks + 2 * me_q] = value[:, :TILE]
        src[b][blocks + 2 * me_q + 1] = value[:, TILE:]

    def halo_wait(b, parts=range(4)):
        for n in parts:
            here = src[b].at[pl.ds(blocks, 2 if n == 3 else 4)]
            copy_to_node(here, here, h_ss.at[b], h_rs.at[b, n], mate).wait_recv()

    def lower(g):
        def step(t, _):
            low[t] = g[:, lanes(t, TILE)].astype(BF16)
            return 0

        lax.fori_loop(0, blocks, step, 0)

    def terms():
        segs[0] = jnp.zeros((total, TILE), F32)

        def step(j, _):
            acc = segs[TERM_UNROLL * j]
            for n in range(TERM_UNROLL):
                i = TERM_UNROLL * j + n
                part = dot(low[lax.rem(plan[0, i], blocks)], adj_sorted[i])
                acc = part + plan[1, i].astype(F32) * acc
                segs[i + 1] = acc
            return 0

        lax.fori_loop(0, slots // TERM_UNROLL, step, 0)

    def rim_send(b, early_rows=False):
        def rim(p):
            tiles = [segs[plan[2, blocks + 2 * p + s]] for s in range(2)]
            return jnp.concatenate(tiles, axis=1).astype(BF16)

        rows16 = pl.ds(pl.multiple_of(lax.div(me_f, 2) * 2 * width, 2 * width), 2 * width)
        for n, shift in enumerate(node_shifts):
            p = node_peer(shift)
            rim_out[b, p] = rim(p)
            if early_rows:
                copy_to_node(rim_out.at[b, p, rows16], own_in.at[me_q], own_sems.at[0], own_sems.at[1], shift).start()
        for n, shift in enumerate(node_shifts):
            p = node_peer(shift)
            copy_to_node(
                rim_out.at[b, p], rim_in.at[b, me_q], r_ss.at[b], r_rs.at[b, n // 2], shift
            ).start()
        if early_rows:
            started.append((own_sems.at[0], own_in.at[pl.ds(0, n_nodes - 1)]))
        started.append((r_ss.at[b], rim_in.at[b, pl.ds(0, n_nodes - 1)]))
        own = rim(me_q)

        def local(c, _):
            tiles = [segs[plan[2, 2 * c + h]] for h in range(2)]
            gm[:, lanes(c)] = jnp.concatenate(tiles, axis=1) + dot(own, spread[me_q, :, lanes(c)])
            return 0

        lax.fori_loop(0, chunks, local, 0, unroll=2)

    def rim_wait(b, n):
        here = rim_in.at[b, pl.ds(0, 1 if n == 3 else 2)]
        copy_to_node(here, here, r_ss.at[b], r_rs.at[b, n], mate).wait_recv()

    def rim_add(b, n):
        rim_wait(b, n)
        peers = [node_peer(back(shift)) for shift in ([mate] if n == 3 else groups[n])]

        def step(c, _):
            acc = gm[:, lanes(c)]
            for p in peers:
                acc = acc + dot(rim_in[b, p], spread[p, :, lanes(c)])
            gm[:, lanes(c)] = acc
            return 0

        lax.fori_loop(0, chunks, step, 0, unroll=2)

    def pull_back(b, layer, group, g, last=True):
        if last:
            rim_wait(b, 2)
            peers = [node_peer(back(shift)) for shift in groups[2]]

        def step(c, _):
            acc = gm[:, lanes(c)]
            if last:
                for p in peers:
                    acc = acc + dot(rim_in[b, p], spread[p, :, lanes(c)])
            value = acc.astype(BF16)
            gml[:, lanes(c)] = value
            gnorm = dot(weights_ref[layer, group], value) * dgate[b, :, lanes(c)]
            norm = normed[b, :, lanes(c)]
            first = jnp.sum(gnorm, axis=0, keepdims=True) * (1.0 / total)
            second = jnp.sum(gnorm * norm, axis=0, keepdims=True) * (1.0 / total)
            state = g[:, lanes(c)] + inverse[b, :, lanes(c)] * (gnorm - first - norm * second)
            g[:, lanes(c)] = state
            state = state.astype(BF16)
            low[2 * c] = state[:, :TILE]
            low[2 * c + 1] = state[:, TILE:]
            return 0

        lax.fori_loop(0, chunks, step, 0, unroll=2)

    puts = []

    def put(source, target, n):
        copy = pltpu.make_async_copy(source, target, out_sems.at[n])
        copy.start()
        puts.append(copy)

    def early_weight_rows():
        here = own_in.at[pl.ds(0, n_nodes - 1)]
        copy_to_node(here, here, own_sems.at[0], own_sems.at[1], mate).wait_recv()
        rows16 = pl.ds(pl.multiple_of(lax.div(me_f, 2) * 2 * width, 2 * width), 2 * width)
        peers = [node_peer(shift) for shift in node_shifts]

        def step(c, _):
            acc = gm[rows16, lanes(c)]
            for p in peers:
                acc = acc + dot(own_in[p], spread[p, :, lanes(c)])
            gml16[:, lanes(c)] = acc.astype(BF16)
            return 0

        lax.fori_loop(0, chunks, step, 0, unroll=2)
        weight_send(0, gml16[...])

    def weight_send(b, own=None):
        if own is None:
            own = gml[pl.ds(pl.multiple_of(lax.div(me_f, 2) * 2 * width, 2 * width), 2 * width), :]
        part = dot_nt(own, activ[b])
        part = jnp.where(lax.rem(me_f, 2) == 0, part[:width], part[width:])
        gw_send[b] = part
        gw_recv[b, me_q] = part
        for shift in node_shifts:
            copy_to_node(gw_send.at[b], gw_recv.at[b, me_q], w_ss.at[b], w_rs.at[b], shift).start()

    def mine(ref):
        return ref[pl.ds(pl.multiple_of(me_f * width, width), width), :]

    take_gathered(0)
    forward(0, 0, 0, x2)
    halo_send(0)
    relay_lines(1)
    relay_lines(2)
    relay_lines(3)
    gates(0)
    take_gathered(1)
    halo_wait(0)
    aggregate(0, x1)

    forward(1, 0, 1, x1)
    halo_send(1)
    gates(1)
    take_gathered(2)
    lower(g2)
    terms()
    rim_send(3)
    halo_wait(1)
    aggregate(1, x2)

    forward(2, 1, 0, x2)
    halo_send(2)
    gates(2)
    take_gathered(3)
    rim_add(3, 3)
    rim_add(3, 0)
    rim_add(3, 1)
    rim_add(3, 2)
    halo_wait(2)
    aggregate(2, x1)

    forward(3, 1, 1, x1, with_gate=True)
    pull_back(3, 1, 1, g1, last=False)
    terms()
    rim_send(2)
    weight_send(3)
    halo_send(3)
    out_ref[0] = mine(x1)
    put(out_ref.at[0], out_hbm.at[0], 0)
    rim_add(2, 3)
    rim_add(2, 0)
    rim_add(2, 1)
    pull_back(2, 1, 0, g2)

    terms()
    rim_send(1)
    weight_send(2)
    halo_wait(3)
    aggregate(3, x2)
    out_ref[1] = mine(x2)
    put(out_ref.at[1], out_hbm.at[1], 1)
    rim_add(1, 3)
    rim_add(1, 0)
    rim_add(1, 1)
    pull_back(1, 0, 1, g1)

    terms()
    rim_send(0, early_rows=True)
    weight_send(1)
    sg_ref[0] = mine(g1)
    put(sg_ref.at[0], sg_hbm.at[0], 2)
    early_weight_rows()
    rim_add(0, 3)
    rim_add(0, 0)
    rim_add(0, 1)
    pull_back(0, 0, 0, g2)
    sg_ref[1] = mine(g2)
    put(sg_ref.at[1], sg_hbm.at[1], 3)

    for b in range(4):
        here = gw_recv.at[b, pl.ds(0, n_nodes - 1)]
        pltpu.make_async_remote_copy(
            src_ref=here, dst_ref=here, send_sem=w_ss.at[b], recv_sem=w_rs.at[b],
            device_id=(node_peer(mate), me_f), device_id_type=MESH,
        ).wait()
        summed = gw_recv[b, 0]
        for p in range(1, n_nodes):
            summed = summed + gw_recv[b, p]
        wg_ref[b // 2, b % 2] = summed
        if b == 3:
            put(wg_ref, wg_hbm, 4)
    for sends, here in started_feat:
        copy_to_feat(here, here, sends, ag_rs.at[0], (0, 1)).wait_send()
    for sends, here in started:
        copy_to_node(here, here, sends, w_rs.at[0], mate).wait_send()
    for copy in puts:
        copy.wait()


def hand_over(out, sg, wg, out_ref, sg_ref, wg_ref):
    out_ref[...] = out[...]
    sg_ref[...] = sg[...]
    wg_ref[...] = wg[...]


def solution(mesh):
    n_nodes, n_feat = mesh.shape["nodes"], mesh.shape["feat"]

    def body(node_states, weights, adj_tiles, tile_source, tile_count, send_rows, send_count, out_grads):
        groups, width, rows = node_states.shape
        total = width * n_feat
        blocks, depth = tile_source.shape
        slots = send_rows.shape[2]
        source_tiles = blocks + n_nodes * slots // TILE
        vmem = pl.BlockSpec(memory_space=pltpu.VMEM)
        smem = pl.BlockSpec(memory_space=pltpu.SMEM)
        hbm = pl.BlockSpec(memory_space=pl.ANY)
        dma = pltpu.SemaphoreType.DMA((4,))
        outs = pl.pallas_call(
            functools.partial(kernel, n_nodes, n_feat),
            out_shape=(
                jax.ShapeDtypeStruct(node_states.shape, F32),
                jax.ShapeDtypeStruct(out_grads.shape, F32),
                jax.ShapeDtypeStruct((2, 2, width, total), F32),
            ),
            in_specs=[hbm] * 5 + [smem] * 3,
            out_specs=(hbm,) * 3,
            scratch_shapes=[
                pltpu.VMEM(node_states.shape, F32),
                pltpu.VMEM(out_grads.shape, F32),
                pltpu.VMEM(weights.shape, BF16),
                pltpu.VMEM(send_rows.shape, jnp.int32),
                pltpu.VMEM(node_states.shape, F32),
                pltpu.VMEM(out_grads.shape, F32),
                pltpu.VMEM((2, 2, width, total), F32),
                pltpu.VMEM(adj_tiles.shape, BF16),
                pltpu.VMEM((8, TILE), jnp.int32),
                pltpu.SMEM((8, TILE), jnp.int32),
                pltpu.SemaphoreType.DMA((6,)),
                pltpu.VMEM((2 * width, rows // 2), BF16),
                pltpu.VMEM((n_feat, 2 * width, rows // 2), BF16),
                pltpu.VMEM((3, 2, 2 * width, rows // 4), BF16),
                pltpu.VMEM((3, 2, 4, n_feat // 4, 2 * width, rows // 4), BF16),
                pltpu.SemaphoreType.DMA((4, 4)),
                pltpu.SemaphoreType.DMA((4, 4)),
                pltpu.VMEM((total, rows), F32),
                pltpu.VMEM((total, rows), F32),
                pltpu.VMEM((total, rows), F32),
                pltpu.VMEM((total, rows), F32),
                pltpu.VMEM((2, 2, total, total), BF16),
                pltpu.VMEM((blocks, depth * TILE, TILE), BF16),
                pltpu.VMEM((blocks * depth, TILE, TILE), BF16),
                pltpu.VMEM((n_nodes, rows, slots), BF16),
                pltpu.VMEM((n_nodes, slots, rows), BF16),
                pltpu.VMEM((4, total, rows), F32),
                pltpu.VMEM((4, total, rows), F32),
                pltpu.VMEM((4, total, rows), BF16),
                pltpu.VMEM((4, 1, rows), F32),
                pltpu.VMEM((total, rows), BF16),
                *[pltpu.VMEM((source_tiles, total, TILE), BF16)] * 4,
                pltpu.VMEM((4, n_nodes, 2, total, TILE), BF16),
                pltpu.VMEM((blocks, total, TILE), BF16),
                pltpu.VMEM((blocks * depth + 1, total, TILE), F32),
                pltpu.VMEM((4, n_nodes, total, slots), BF16),
                pltpu.VMEM((4, n_nodes, total, slots), BF16),
                pltpu.VMEM((total, rows), F32),
                pltpu.VMEM((total, rows), BF16),
                pltpu.VMEM((4, width, total), F32),
                pltpu.VMEM((4, n_nodes, width, total), F32),
                pltpu.VMEM((n_nodes, 2 * width, slots), BF16),
                pltpu.VMEM((2 * width, rows), BF16),
                pltpu.SemaphoreType.DMA((5,)),
                dma, dma, dma, pltpu.SemaphoreType.DMA((4, 4)), dma, pltpu.SemaphoreType.DMA((4, 4)), dma, dma,
                pltpu.SemaphoreType.DMA((2,)),
            ],
            compiler_params=pltpu.CompilerParams(
                collective_id=0, has_side_effects=True, vmem_limit_bytes=62 * 2**20
            ),
        )(
            node_states, out_grads, weights, adj_tiles, send_rows,
            tile_source.T, tile_count, send_count,
        )
        outs = pl.pallas_call(
            hand_over,
            out_shape=tuple(jax.ShapeDtypeStruct(o.shape, o.dtype) for o in outs),
            in_specs=[vmem] * 3,
            out_specs=(vmem,) * 3,
        )(*outs)
        return outs[0], outs[1], jnp.swapaxes(outs[2], 2, 3)

    return jax.shard_map(
        body,
        mesh=mesh,
        in_specs=(
            P(None, "feat", "nodes"),
            P(),
            P("nodes", None, None, None),
            P("nodes", None),
            P("nodes"),
            P("nodes", None, None),
            P("nodes", None),
            P(None, "feat", "nodes"),
        ),
        out_specs=(P(None, "feat", "nodes"), P(None, "feat", "nodes"), P(None, None, None, "feat")),
        check_vma=False,
    )
```

```python
import functools

import jax
import jax.numpy as jnp
from jax import lax
from jax.experimental import pallas as pl
from jax.experimental.pallas import tpu as pltpu
from jax.sharding import PartitionSpec as P

MESH = pl.DeviceIdType.MESH
TILE = 128
EPS = 1e-05
TERM_UNROLL = 32
F32 = jnp.float32
BF16 = jnp.bfloat16


def dot(a, b):
    return jnp.dot(a, b, preferred_element_type=F32)


def dot_nt(a, b):
    return lax.dot_general(a, b, (((1,), (1,)), ((), ())), preferred_element_type=F32)


def kernel(
    n_nodes, n_feat,
    states_hbm, grads_hbm, weights_hbm, adj_hbm, rows_hbm,
    source_ref, count_ref, sent_ref,
    out_hbm, sg_hbm, wg_hbm,
    states_ref, grads_ref, weights_ref, rows_ref, out_ref, sg_ref, wg_ref,
    adj_ref, plan_rows, plan, local_sems,
    ag_send, ag_recv, line_send, line_recv, line_ss, line_rs, x1, x2, g1, g2, wt,
    fwd_tiles, adj_sorted, pick, spread,
    normed, dgate, activ, inverse, mixed,
    src0, src1, src2, src3, halo_out, low, segs, rim_out, rim_in, gm, gml,
    gw_send, gw_recv, own_in, gml16, out_sems,
    ag_ss, ag_rs, h_ss, h_rs, r_ss, r_rs, w_ss, w_rs, own_sems,
):
    src = (src0, src1, src2, src3)
    me_q = lax.axis_index("nodes")
    me_f = lax.axis_index("feat")
    width = states_ref.shape[1]
    rows = states_ref.shape[2]
    total = width * n_feat
    half = rows // 2
    blocks = rows // TILE
    chunks = rows // 256
    depth = adj_ref.shape[1]
    slots = blocks * depth

    me_x, me_c = lax.div(me_q, 2), lax.rem(me_q, 2)
    me_z, me_y = lax.div(me_f, 4), lax.rem(me_f, 4)

    def node_peer(shift):
        dx, dc = shift
        return lax.rem(me_x + dx, n_nodes // 2) * 2 + lax.rem(me_c + dc, 2)

    def feat_peer(shift):
        dz, dy = shift
        return lax.rem(me_z + dz, n_feat // 4) * 4 + lax.rem(me_y + dy, 4)

    def hops(shift):
        return min(shift[0], 4 - shift[0]) + min(shift[1], 4 - shift[1])

    feat_shifts = [(dz, dy) for dz in range(4) for dy in range(4) if dz or dy]
    feat_shifts.sort(key=lambda shift: -hops(shift))
    mate = (0, 1)
    groups = [((2, 0), (2, 1)), ((1, 0), (3, 0)), ((1, 1), (3, 1))]
    far_shifts = [shift for group in groups for shift in group]
    node_shifts = far_shifts + [mate]

    def back(shift):
        return ((4 - shift[0]) % 4, shift[1])

    started = []
    started_feat = []
    barrier = pltpu.get_barrier_semaphore()
    for shift in feat_shifts:
        pl.semaphore_signal(barrier, inc=1, device_id=(me_q, feat_peer(shift)), device_id_type=MESH)
    for shift in node_shifts:
        pl.semaphore_signal(barrier, inc=1, device_id=(node_peer(shift), me_f), device_id_type=MESH)

    states_copy = pltpu.make_async_copy(states_hbm, states_ref, local_sems.at[2])
    grads_copy = pltpu.make_async_copy(grads_hbm, grads_ref, local_sems.at[3])
    rows_copy = pltpu.make_async_copy(rows_hbm, rows_ref, local_sems.at[4])
    weights_copy = pltpu.make_async_copy(weights_hbm, weights_ref, local_sems.at[5])
    adj_copy = pltpu.make_async_copy(adj_hbm, adj_ref, local_sems.at[0])
    for copy in (states_copy, grads_copy, rows_copy, weights_copy, adj_copy):
        copy.start()
    states_copy.wait()
    grads_copy.wait()

    gathered = [(states_ref, 1, x2), (states_ref, 0, x1), (grads_ref, 1, g2), (grads_ref, 0, g1)]
    for a, (ref, group, _) in enumerate(gathered):
        packed = jnp.concatenate([ref[group, :, :half], ref[group, :, half:]], axis=0).astype(BF16)
        if a == 0:
            ag_send[...] = packed
            ag_recv[me_f] = packed
        else:
            quarter = half // 2
            line_send[a - 1, 0] = packed[:, :quarter]
            line_send[a - 1, 1] = packed[:, quarter:]
            line_recv[a - 1, 0, me_z, me_y] = packed[:, :quarter]
            line_recv[a - 1, 1, me_y, me_z] = packed[:, quarter:]
    weights_copy.wait()
    for layer in range(2):
        for group in range(2):
            wt[layer, group] = weights_ref[layer, group].astype(F32).T.astype(BF16)

    lane = lax.broadcasted_iota(jnp.int32, (1, TILE), 1)
    source = jnp.full((1, TILE), blocks * TILE, jnp.int32)
    for e in range(slots):
        source = jnp.where(lane == e, source_ref[e // blocks, e % blocks], source)
    place = lax.broadcasted_iota(jnp.int32, (TILE, TILE), 0)
    lanes_of = lax.broadcasted_iota(jnp.int32, (TILE, TILE), 1)

    def column(row):
        return jnp.broadcast_to(row, (TILE, TILE)).T

    source_column = column(source)
    key = source * TILE + lane
    rank = column(jnp.sum((column(key) < key).astype(jnp.int32), axis=0, keepdims=True))
    at = rank == lanes_of
    before = rank + 1 == lanes_of
    order = jnp.sum(jnp.where(at, place, 0), axis=0, keepdims=True)
    ordered = jnp.sum(jnp.where(at, source_column, 0), axis=0, keepdims=True)
    previous = jnp.sum(jnp.where(before, source_column, 0), axis=0, keepdims=True)
    keep = jnp.where((ordered == previous) & (lane > 0), 1, 0)
    upto = jnp.sum((source_column <= lanes_of).astype(jnp.int32), axis=0, keepdims=True)
    has = jnp.sum((source_column == lanes_of).astype(jnp.int32), axis=0, keepdims=True)
    plan_rows[0:1, :] = order
    plan_rows[1:2, :] = keep
    plan_rows[2:3, :] = jnp.where(has > 0, upto, 0)
    plan_copy = pltpu.make_async_copy(plan_rows, plan, local_sems.at[1])
    plan_copy.start()

    def prepare_block(t, _):
        for k in range(depth):
            keep = (k < count_ref[t]).astype(F32)
            tile = adj_ref[t, k].astype(F32) * keep
            fwd_tiles[t, k * TILE:(k + 1) * TILE, :] = tile.T.astype(BF16)
        return 0

    adj_copy.wait()
    lax.fori_loop(0, blocks, prepare_block, 0)

    def prepare_sorted(i, _):
        e = plan[0, i]
        t = lax.rem(e, blocks)
        k = lax.div(e, blocks)
        keep = (k < count_ref[t]).astype(F32)
        adj_sorted[i] = (adj_ref[t, k].astype(F32) * keep).astype(BF16)
        return 0

    plan_copy.wait()
    lax.fori_loop(0, slots, prepare_sorted, 0)

    def prepare_pick(p, _):
        lane = lax.broadcasted_iota(jnp.int32, (1, 256), 1)
        index = jnp.where(lane < sent_ref[0, p], rows_ref[0, pl.ds(p, 1), :], -1)
        high = lax.broadcasted_iota(jnp.int32, (256, 256), 0)
        for c in range(chunks):
            hit = high + c * 256 == index
            pick[p, c * 256:(c + 1) * 256, :] = jnp.where(hit, 1.0, 0.0).astype(BF16)
        value = index.astype(F32)
        place = lax.broadcasted_iota(jnp.int32, (TILE, 256), 1).astype(F32)
        for s in range(2):
            column = jnp.broadcast_to(value[:, s * TILE:(s + 1) * TILE], (TILE, TILE)).T
            column = jnp.concatenate([column, column], axis=1)
            for c in range(chunks):
                hit = place + float(c * 256) == column
                spread[p, s * TILE:(s + 1) * TILE, c * 256:(c + 1) * 256] = jnp.where(hit, 1.0, 0.0).astype(BF16)
        return 0

    rows_copy.wait()
    lax.fori_loop(0, n_nodes, prepare_pick, 0)

    pl.semaphore_wait(barrier, n_feat - 1 + n_nodes - 1)

    def copy_to_feat(source, target, sends, receives, shift):
        return pltpu.make_async_remote_copy(
            src_ref=source, dst_ref=target, send_sem=sends, recv_sem=receives,
            device_id=(me_q, feat_peer(shift)), device_id_type=MESH,
        )

    lines = ([(0, 2), (0, 1), (0, 3)], [(2, 0), (1, 0), (3, 0)])
    place_of = ((me_z, me_y), (me_y, me_z))

    def send_direct():
        for shift in feat_shifts:
            copy_to_feat(ag_send, ag_recv.at[me_f], ag_ss.at[0], ag_rs.at[0], shift).start()
        started_feat.append((ag_ss.at[0], ag_recv.at[pl.ds(0, n_feat - 1)]))

    def send_lines(a):
        for w in range(2):
            first, second = place_of[w]
            for shift in lines[w]:
                copy_to_feat(
                    line_send.at[a - 1, w], line_recv.at[a - 1, w, first, second],
                    line_ss.at[a, w], line_rs.at[a, w], shift,
                ).start()
            started_feat.append((line_ss.at[a, w], line_recv.at[a - 1, w, 0, pl.ds(0, 3)]))

    def relay_lines(a):
        for w in range(2):
            here = line_recv.at[a - 1, w, 0, pl.ds(0, 3)]
            copy_to_feat(here, here, line_ss.at[a, w], line_rs.at[a, w], (0, 1)).wait_recv()
            first = place_of[w][0]
            for shift in lines[1 - w]:
                copy_to_feat(
                    line_recv.at[a - 1, w, first], line_recv.at[a - 1, w, first],
                    line_ss.at[a, 2 + w], line_rs.at[a, 2 + w], shift,
                ).start()
            started_feat.append((line_ss.at[a, 2 + w], line_recv.at[a - 1, w, pl.ds(0, 3)]))

    send_direct()
    for a in range(1, 4):
        send_lines(a)

    def take_gathered(a):
        ref, group, target = gathered[a]
        if a == 0:
            here = ag_recv.at[pl.ds(0, n_feat - 1)]
            copy_to_feat(here, here, ag_ss.at[0], ag_rs.at[0], (0, 1)).wait_recv()
            for f in range(n_feat):
                got = ag_recv[f].astype(F32)
                target[f * width:(f + 1) * width, :half] = got[:width]
                target[f * width:(f + 1) * width, half:] = got[width:]
        else:
            quarter = half // 2
            for w in range(2):
                here = line_recv.at[a - 1, w, pl.ds(0, 3)]
                copy_to_feat(here, here, line_ss.at[a, 2 + w], line_rs.at[a, 2 + w], (0, 1)).wait_recv()
                for f in range(n_feat):
                    z, y = f // 4, f % 4
                    got = line_recv[a - 1, w, (z, y)[w], (y, z)[w]].astype(F32)
                    at = w * quarter
                    target[f * width:(f + 1) * width, at:at + quarter] = got[:width]
                    target[f * width:(f + 1) * width, half + at:half + at + quarter] = got[width:]
        target[pl.ds(pl.multiple_of(me_f * width, width), width), :] = ref[group]

    def lanes(c, size=256):
        return pl.ds(pl.multiple_of(c * size, size), size)

    def copy_to_node(source, target, sends, receives, shift):
        return pltpu.make_async_remote_copy(
            src_ref=source, dst_ref=target, send_sem=sends, recv_sem=receives,
            device_id=(node_peer(shift), me_f), device_id_type=MESH,
        )

    def forward(b, layer, group, u, with_gate=False):
        def step(c, _):
            states = u[:, lanes(c)]
            center = jnp.sum(states, axis=0, keepdims=True) * (1.0 / total)
            square = jnp.sum(states * states, axis=0, keepdims=True) * (1.0 / total)
            inv = lax.rsqrt(square - center * center + EPS)
            norm = (states - center) * inv
            gate = 1.0 / (1.0 + jnp.exp(-norm))
            normed[b, :, lanes(c)] = norm
            inverse[b, :, lanes(c)] = inv
            act = (norm * gate).astype(BF16)
            activ[b, :, lanes(c)] = act
            if with_gate:
                dgate[b, :, lanes(c)] = gate * (1.0 + norm * (1.0 - gate))
            value = dot(wt[layer, group], act).astype(BF16)
            mixed[:, lanes(c)] = value
            src[b][2 * c] = value[:, :TILE]
            src[b][2 * c + 1] = value[:, TILE:]
            return 0

        lax.fori_loop(0, chunks, step, 0, unroll=8)

    def aggregate(b, u):
        def step(t, _):
            tiles = [src[b][source_ref[k, t]] for k in range(depth)]
            u[:, lanes(t, TILE)] += dot(jnp.concatenate(tiles, axis=1), fwd_tiles[t])
            return 0

        lax.fori_loop(0, blocks, step, 0, unroll=16)

    def gates(b):
        def step(c, _):
            norm = normed[b, :, lanes(c)]
            gate = 1.0 / (1.0 + jnp.exp(-norm))
            dgate[b, :, lanes(c)] = gate * (1.0 + norm * (1.0 - gate))
            return 0

        lax.fori_loop(0, chunks, step, 0)

    def halo_send(b):
        for n, shift in enumerate(node_shifts):
            p = node_peer(shift)
            value = dot(mixed[...], pick[p]).astype(BF16)
            halo_out[b, p, 0] = value[:, :TILE]
            halo_out[b, p, 1] = value[:, TILE:]
            copy_to_node(
                halo_out.at[b, p], src[b].at[pl.ds(blocks + 2 * me_q, 2)], h_ss.at[b], h_rs.at[b, n // 2], shift
            ).start()
        started.append((h_ss.at[b], src[b].at[pl.ds(blocks, 2 * (n_nodes - 1))]))
        value = dot(mixed[...], pick[me_q]).astype(BF16)
        src[b][blocks + 2 * me_q] = value[:, :TILE]
        src[b][blocks + 2 * me_q + 1] = value[:, TILE:]

    def halo_wait(b, parts=range(4)):
        for n in parts:
            here = src[b].at[pl.ds(blocks, 2 if n == 3 else 4)]
            copy_to_node(here, here, h_ss.at[b], h_rs.at[b, n], mate).wait_recv()

    def lower(g):
        def step(t, _):
            low[t] = g[:, lanes(t, TILE)].astype(BF16)
            return 0

        lax.fori_loop(0, blocks, step, 0)

    def terms():
        segs[0] = jnp.zeros((total, TILE), F32)

        def step(j, _):
            acc = segs[TERM_UNROLL * j]
            for n in range(TERM_UNROLL):
                i = TERM_UNROLL * j + n
                part = dot(low[lax.rem(plan[0, i], blocks)], adj_sorted[i])
                acc = part + plan[1, i].astype(F32) * acc
                segs[i + 1] = acc
            return 0

        lax.fori_loop(0, slots // TERM_UNROLL, step, 0)

    def rim_send(b, early_rows=False):
        def rim(p):
            tiles = [segs[plan[2, blocks + 2 * p + s]] for s in range(2)]
            return jnp.concatenate(tiles, axis=1).astype(BF16)

        rows16 = pl.ds(pl.multiple_of(lax.div(me_f, 2) * 2 * width, 2 * width), 2 * width)
        for n, shift in enumerate(node_shifts):
            p = node_peer(shift)
            rim_out[b, p] = rim(p)
            if early_rows:
                copy_to_node(rim_out.at[b, p, rows16], own_in.at[me_q], own_sems.at[0], own_sems.at[1], shift).start()
        for n, shift in enumerate(node_shifts):
            p = node_peer(shift)
            copy_to_node(
                rim_out.at[b, p], rim_in.at[b, me_q], r_ss.at[b], r_rs.at[b, n // 2], shift
            ).start()
        if early_rows:
            started.append((own_sems.at[0], own_in.at[pl.ds(0, n_nodes - 1)]))
        started.append((r_ss.at[b], rim_in.at[b, pl.ds(0, n_nodes - 1)]))
        own = rim(me_q)

        def local(c, _):
            tiles = [segs[plan[2, 2 * c + h]] for h in range(2)]
            gm[:, lanes(c)] = jnp.concatenate(tiles, axis=1) + dot(own, spread[me_q, :, lanes(c)])
            return 0

        lax.fori_loop(0, chunks, local, 0, unroll=2)

    def rim_wait(b, n):
        here = rim_in.at[b, pl.ds(0, 1 if n == 3 else 2)]
        copy_to_node(here, here, r_ss.at[b], r_rs.at[b, n], mate).wait_recv()

    def rim_add(b, n):
        rim_wait(b, n)
        peers = [node_peer(back(shift)) for shift in ([mate] if n == 3 else groups[n])]

        def step(c, _):
            acc = gm[:, lanes(c)]
            for p in peers:
                acc = acc + dot(rim_in[b, p], spread[p, :, lanes(c)])
            gm[:, lanes(c)] = acc
            return 0

        lax.fori_loop(0, chunks, step, 0, unroll=2)

    def pull_back(b, layer, group, g, last=True):
        if last:
            rim_wait(b, 2)
            peers = [node_peer(back(shift)) for shift in groups[2]]

        def step(c, _):
            acc = gm[:, lanes(c)]
            if last:
                for p in peers:
                    acc = acc + dot(rim_in[b, p], spread[p, :, lanes(c)])
            value = acc.astype(BF16)
            gml[:, lanes(c)] = value
            gnorm = dot(weights_ref[layer, group], value) * dgate[b, :, lanes(c)]
            norm = normed[b, :, lanes(c)]
            first = jnp.sum(gnorm, axis=0, keepdims=True) * (1.0 / total)
            second = jnp.sum(gnorm * norm, axis=0, keepdims=True) * (1.0 / total)
            state = g[:, lanes(c)] + inverse[b, :, lanes(c)] * (gnorm - first - norm * second)
            g[:, lanes(c)] = state
            state = state.astype(BF16)
            low[2 * c] = state[:, :TILE]
            low[2 * c + 1] = state[:, TILE:]
            return 0

        lax.fori_loop(0, chunks, step, 0, unroll=4)

    puts = []

    def put(source, target, n):
        copy = pltpu.make_async_copy(source, target, out_sems.at[n])
        copy.start()
        puts.append(copy)

    def early_weight_rows():
        here = own_in.at[pl.ds(0, n_nodes - 1)]
        copy_to_node(here, here, own_sems.at[0], own_sems.at[1], mate).wait_recv()
        rows16 = pl.ds(pl.multiple_of(lax.div(me_f, 2) * 2 * width, 2 * width), 2 * width)
        peers = [node_peer(shift) for shift in node_shifts]

        def step(c, _):
            acc = gm[rows16, lanes(c)]
            for p in peers:
                acc = acc + dot(own_in[p], spread[p, :, lanes(c)])
            gml16[:, lanes(c)] = acc.astype(BF16)
            return 0

        lax.fori_loop(0, chunks, step, 0, unroll=2)
        weight_send(0, gml16[...])

    def weight_send(b, own=None):
        if own is None:
            own = gml[pl.ds(pl.multiple_of(lax.div(me_f, 2) * 2 * width, 2 * width), 2 * width), :]
        part = dot_nt(own, activ[b])
        part = jnp.where(lax.rem(me_f, 2) == 0, part[:width], part[width:])
        gw_send[b] = part
        gw_recv[b, me_q] = part
        for shift in node_shifts:
            copy_to_node(gw_send.at[b], gw_recv.at[b, me_q], w_ss.at[b], w_rs.at[b], shift).start()

    def mine(ref):
        return ref[pl.ds(pl.multiple_of(me_f * width, width), width), :]

    take_gathered(0)
    forward(0, 0, 0, x2)
    halo_send(0)
    relay_lines(1)
    relay_lines(2)
    relay_lines(3)
    gates(0)
    take_gathered(1)
    halo_wait(0)
    aggregate(0, x1)

    forward(1, 0, 1, x1)
    halo_send(1)
    gates(1)
    take_gathered(2)
    lower(g2)
    terms()
    rim_send(3)
    halo_wait(1)
    aggregate(1, x2)

    forward(2, 1, 0, x2)
    halo_send(2)
    gates(2)
    take_gathered(3)
    rim_add(3, 3)
    rim_add(3, 0)
    rim_add(3, 1)
    rim_add(3, 2)
    halo_wait(2)
    aggregate(2, x1)

    forward(3, 1, 1, x1, with_gate=True)
    pull_back(3, 1, 1, g1, last=False)
    terms()
    rim_send(2)
    weight_send(3)
    halo_send(3)
    out_ref[0] = mine(x1)
    put(out_ref.at[0], out_hbm.at[0], 0)
    rim_add(2, 3)
    rim_add(2, 0)
    rim_add(2, 1)
    pull_back(2, 1, 0, g2)

    terms()
    rim_send(1)
    weight_send(2)
    halo_wait(3)
    aggregate(3, x2)
    out_ref[1] = mine(x2)
    put(out_ref.at[1], out_hbm.at[1], 1)
    rim_add(1, 3)
    rim_add(1, 0)
    rim_add(1, 1)
    pull_back(1, 0, 1, g1)

    terms()
    rim_send(0, early_rows=True)
    weight_send(1)
    sg_ref[0] = mine(g1)
    put(sg_ref.at[0], sg_hbm.at[0], 2)
    early_weight_rows()
    rim_add(0, 3)
    rim_add(0, 0)
    rim_add(0, 1)
    pull_back(0, 0, 0, g2)
    sg_ref[1] = mine(g2)
    put(sg_ref.at[1], sg_hbm.at[1], 3)

    for b in range(4):
        here = gw_recv.at[b, pl.ds(0, n_nodes - 1)]
        pltpu.make_async_remote_copy(
            src_ref=here, dst_ref=here, send_sem=w_ss.at[b], recv_sem=w_rs.at[b],
            device_id=(node_peer(mate), me_f), device_id_type=MESH,
        ).wait()
        summed = gw_recv[b, 0]
        for p in range(1, n_nodes):
            summed = summed + gw_recv[b, p]
        wg_ref[b // 2, b % 2] = summed
        if b == 3:
            put(wg_ref, wg_hbm, 4)
    for sends, here in started_feat:
        copy_to_feat(here, here, sends, ag_rs.at[0], (0, 1)).wait_send()
    for sends, here in started:
        copy_to_node(here, here, sends, w_rs.at[0], mate).wait_send()
    for copy in puts:
        copy.wait()


def hand_over(out, sg, wg, out_ref, sg_ref, wg_ref):
    out_ref[...] = out[...]
    sg_ref[...] = sg[...]
    wg_ref[...] = wg[...]


def solution(mesh):
    n_nodes, n_feat = mesh.shape["nodes"], mesh.shape["feat"]

    def body(node_states, weights, adj_tiles, tile_source, tile_count, send_rows, send_count, out_grads):
        groups, width, rows = node_states.shape
        total = width * n_feat
        blocks, depth = tile_source.shape
        slots = send_rows.shape[2]
        source_tiles = blocks + n_nodes * slots // TILE
        vmem = pl.BlockSpec(memory_space=pltpu.VMEM)
        smem = pl.BlockSpec(memory_space=pltpu.SMEM)
        hbm = pl.BlockSpec(memory_space=pl.ANY)
        dma = pltpu.SemaphoreType.DMA((4,))
        outs = pl.pallas_call(
            functools.partial(kernel, n_nodes, n_feat),
            out_shape=(
                jax.ShapeDtypeStruct(node_states.shape, F32),
                jax.ShapeDtypeStruct(out_grads.shape, F32),
                jax.ShapeDtypeStruct((2, 2, width, total), F32),
            ),
            in_specs=[hbm] * 5 + [smem] * 3,
            out_specs=(hbm,) * 3,
            scratch_shapes=[
                pltpu.VMEM(node_states.shape, F32),
                pltpu.VMEM(out_grads.shape, F32),
                pltpu.VMEM(weights.shape, BF16),
                pltpu.VMEM(send_rows.shape, jnp.int32),
                pltpu.VMEM(node_states.shape, F32),
                pltpu.VMEM(out_grads.shape, F32),
                pltpu.VMEM((2, 2, width, total), F32),
                pltpu.VMEM(adj_tiles.shape, BF16),
                pltpu.VMEM((8, TILE), jnp.int32),
                pltpu.SMEM((8, TILE), jnp.int32),
                pltpu.SemaphoreType.DMA((6,)),
                pltpu.VMEM((2 * width, rows // 2), BF16),
                pltpu.VMEM((n_feat, 2 * width, rows // 2), BF16),
                pltpu.VMEM((3, 2, 2 * width, rows // 4), BF16),
                pltpu.VMEM((3, 2, 4, n_feat // 4, 2 * width, rows // 4), BF16),
                pltpu.SemaphoreType.DMA((4, 4)),
                pltpu.SemaphoreType.DMA((4, 4)),
                pltpu.VMEM((total, rows), F32),
                pltpu.VMEM((total, rows), F32),
                pltpu.VMEM((total, rows), F32),
                pltpu.VMEM((total, rows), F32),
                pltpu.VMEM((2, 2, total, total), BF16),
                pltpu.VMEM((blocks, depth * TILE, TILE), BF16),
                pltpu.VMEM((blocks * depth, TILE, TILE), BF16),
                pltpu.VMEM((n_nodes, rows, slots), BF16),
                pltpu.VMEM((n_nodes, slots, rows), BF16),
                pltpu.VMEM((4, total, rows), F32),
                pltpu.VMEM((4, total, rows), F32),
                pltpu.VMEM((4, total, rows), BF16),
                pltpu.VMEM((4, 1, rows), F32),
                pltpu.VMEM((total, rows), BF16),
                *[pltpu.VMEM((source_tiles, total, TILE), BF16)] * 4,
                pltpu.VMEM((4, n_nodes, 2, total, TILE), BF16),
                pltpu.VMEM((blocks, total, TILE), BF16),
                pltpu.VMEM((blocks * depth + 1, total, TILE), F32),
                pltpu.VMEM((4, n_nodes, total, slots), BF16),
                pltpu.VMEM((4, n_nodes, total, slots), BF16),
                pltpu.VMEM((total, rows), F32),
                pltpu.VMEM((total, rows), BF16),
                pltpu.VMEM((4, width, total), F32),
                pltpu.VMEM((4, n_nodes, width, total), F32),
                pltpu.VMEM((n_nodes, 2 * width, slots), BF16),
                pltpu.VMEM((2 * width, rows), BF16),
                pltpu.SemaphoreType.DMA((5,)),
                dma, dma, dma, pltpu.SemaphoreType.DMA((4, 4)), dma, pltpu.SemaphoreType.DMA((4, 4)), dma, dma,
                pltpu.SemaphoreType.DMA((2,)),
            ],
            compiler_params=pltpu.CompilerParams(
                collective_id=0, has_side_effects=True, vmem_limit_bytes=62 * 2**20
            ),
        )(
            node_states, out_grads, weights, adj_tiles, send_rows,
            tile_source.T, tile_count, send_count,
        )
        outs = pl.pallas_call(
            hand_over,
            out_shape=tuple(jax.ShapeDtypeStruct(o.shape, o.dtype) for o in outs),
            in_specs=[vmem] * 3,
            out_specs=(vmem,) * 3,
        )(*outs)
        return outs[0], outs[1], jnp.swapaxes(outs[2], 2, 3)

    return jax.shard_map(
        body,
        mesh=mesh,
        in_specs=(
            P(None, "feat", "nodes"),
            P(),
            P("nodes", None, None, None),
            P("nodes", None),
            P("nodes"),
            P("nodes", None, None),
            P("nodes", None),
            P(None, "feat", "nodes"),
        ),
        out_specs=(P(None, "feat", "nodes"), P(None, "feat", "nodes"), P(None, None, None, "feat")),
        check_vma=False,
    )
```

```python
import functools

import jax
import jax.numpy as jnp
from jax import lax
from jax.experimental import pallas as pl
from jax.experimental.pallas import tpu as pltpu
from jax.sharding import PartitionSpec as P

MESH = pl.DeviceIdType.MESH
TILE = 128
EPS = 1e-05
TERM_UNROLL = 32
F32 = jnp.float32
BF16 = jnp.bfloat16


def dot(a, b):
    return jnp.dot(a, b, preferred_element_type=F32)


def dot_nt(a, b):
    return lax.dot_general(a, b, (((1,), (1,)), ((), ())), preferred_element_type=F32)


def kernel(
    n_nodes, n_feat,
    states_hbm, grads_hbm, weights_hbm, adj_hbm, rows_hbm,
    source_ref, count_ref, sent_ref,
    out_hbm, sg_hbm, wg_hbm,
    states_ref, grads_ref, weights_ref, rows_ref, out_ref, sg_ref, wg_ref,
    adj_ref, plan_rows, plan, local_sems,
    ag_send, ag_recv, line_send, line_recv, line_ss, line_rs, x1, x2, g1, g2, wt,
    fwd_tiles, adj_sorted, pick, spread,
    normed, dgate, activ, inverse, mixed,
    src0, src1, src2, src3, halo_out, low, segs, rim_out, rim_in, gm, gml,
    gw_send, gw_recv, own_in, gml16, out_sems,
    ag_ss, ag_rs, h_ss, h_rs, r_ss, r_rs, w_ss, w_rs, own_sems,
):
    src = (src0, src1, src2, src3)
    me_q = lax.axis_index("nodes")
    me_f = lax.axis_index("feat")
    width = states_ref.shape[1]
    rows = states_ref.shape[2]
    total = width * n_feat
    half = rows // 2
    blocks = rows // TILE
    chunks = rows // 256
    depth = adj_ref.shape[1]
    slots = blocks * depth

    me_x, me_c = lax.div(me_q, 2), lax.rem(me_q, 2)
    me_z, me_y = lax.div(me_f, 4), lax.rem(me_f, 4)

    def node_peer(shift):
        dx, dc = shift
        return lax.rem(me_x + dx, n_nodes // 2) * 2 + lax.rem(me_c + dc, 2)

    def feat_peer(shift):
        dz, dy = shift
        return lax.rem(me_z + dz, n_feat // 4) * 4 + lax.rem(me_y + dy, 4)

    def hops(shift):
        return min(shift[0], 4 - shift[0]) + min(shift[1], 4 - shift[1])

    feat_shifts = [(dz, dy) for dz in range(4) for dy in range(4) if dz or dy]
    feat_shifts.sort(key=lambda shift: -hops(shift))
    mate = (0, 1)
    groups = [((2, 0), (2, 1)), ((1, 0), (3, 0)), ((1, 1), (3, 1))]
    far_shifts = [shift for group in groups for shift in group]
    node_shifts = far_shifts + [mate]

    def back(shift):
        return ((4 - shift[0]) % 4, shift[1])

    started = []
    started_feat = []
    barrier = pltpu.get_barrier_semaphore()
    for shift in feat_shifts:
        pl.semaphore_signal(barrier, inc=1, device_id=(me_q, feat_peer(shift)), device_id_type=MESH)
    for shift in node_shifts:
        pl.semaphore_signal(barrier, inc=1, device_id=(node_peer(shift), me_f), device_id_type=MESH)

    states_copy = pltpu.make_async_copy(states_hbm, states_ref, local_sems.at[2])
    grads_copy = pltpu.make_async_copy(grads_hbm, grads_ref, local_sems.at[3])
    rows_copy = pltpu.make_async_copy(rows_hbm, rows_ref, local_sems.at[4])
    weights_copy = pltpu.make_async_copy(weights_hbm, weights_ref, local_sems.at[5])
    adj_copy = pltpu.make_async_copy(adj_hbm, adj_ref, local_sems.at[0])
    for copy in (states_copy, grads_copy, rows_copy, weights_copy, adj_copy):
        copy.start()
    states_copy.wait()
    grads_copy.wait()

    gathered = [(states_ref, 1, x2), (states_ref, 0, x1), (grads_ref, 1, g2), (grads_ref, 0, g1)]
    for a, (ref, group, _) in enumerate(gathered):
        packed = jnp.concatenate([ref[group, :, :half], ref[group, :, half:]], axis=0).astype(BF16)
        if a == 0:
            ag_send[...] = packed
            ag_recv[me_f] = packed
        else:
            quarter = half // 2
            line_send[a - 1, 0] = packed[:, :quarter]
            line_send[a - 1, 1] = packed[:, quarter:]
            line_recv[a - 1, 0, me_z, me_y] = packed[:, :quarter]
            line_recv[a - 1, 1, me_y, me_z] = packed[:, quarter:]
    weights_copy.wait()
    for layer in range(2):
        for group in range(2):
            wt[layer, group] = weights_ref[layer, group].astype(F32).T.astype(BF16)

    lane = lax.broadcasted_iota(jnp.int32, (1, TILE), 1)
    source = jnp.full((1, TILE), blocks * TILE, jnp.int32)
    for e in range(slots):
        source = jnp.where(lane == e, source_ref[e // blocks, e % blocks], source)
    place = lax.broadcasted_iota(jnp.int32, (TILE, TILE), 0)
    lanes_of = lax.broadcasted_iota(jnp.int32, (TILE, TILE), 1)

    def column(row):
        return jnp.broadcast_to(row, (TILE, TILE)).T

    source_column = column(source)
    key = source * TILE + lane
    rank = column(jnp.sum((column(key) < key).astype(jnp.int32), axis=0, keepdims=True))
    at = rank == lanes_of
    before = rank + 1 == lanes_of
    order = jnp.sum(jnp.where(at, place, 0), axis=0, keepdims=True)
    ordered = jnp.sum(jnp.where(at, source_column, 0), axis=0, keepdims=True)
    previous = jnp.sum(jnp.where(before, source_column, 0), axis=0, keepdims=True)
    keep = jnp.where((ordered == previous) & (lane > 0), 1, 0)
    upto = jnp.sum((source_column <= lanes_of).astype(jnp.int32), axis=0, keepdims=True)
    has = jnp.sum((source_column == lanes_of).astype(jnp.int32), axis=0, keepdims=True)
    plan_rows[0:1, :] = order
    plan_rows[1:2, :] = keep
    plan_rows[2:3, :] = jnp.where(has > 0, upto, 0)
    plan_copy = pltpu.make_async_copy(plan_rows, plan, local_sems.at[1])
    plan_copy.start()

    def prepare_block(t, _):
        for k in range(depth):
            keep = (k < count_ref[t]).astype(F32)
            tile = adj_ref[t, k].astype(F32) * keep
            fwd_tiles[t, k * TILE:(k + 1) * TILE, :] = tile.T.astype(BF16)
        return 0

    adj_copy.wait()
    lax.fori_loop(0, blocks, prepare_block, 0)

    def prepare_sorted(i, _):
        e = plan[0, i]
        t = lax.rem(e, blocks)
        k = lax.div(e, blocks)
        keep = (k < count_ref[t]).astype(F32)
        adj_sorted[i] = (adj_ref[t, k].astype(F32) * keep).astype(BF16)
        return 0

    plan_copy.wait()
    lax.fori_loop(0, slots, prepare_sorted, 0)

    def prepare_pick(p, _):
        lane = lax.broadcasted_iota(jnp.int32, (1, 256), 1)
        index = jnp.where(lane < sent_ref[0, p], rows_ref[0, pl.ds(p, 1), :], -1)
        high = lax.broadcasted_iota(jnp.int32, (256, 256), 0)
        for c in range(chunks):
            hit = high + c * 256 == index
            pick[p, c * 256:(c + 1) * 256, :] = jnp.where(hit, 1.0, 0.0).astype(BF16)
        value = index.astype(F32)
        place = lax.broadcasted_iota(jnp.int32, (TILE, 256), 1).astype(F32)
        for s in range(2):
            column = jnp.broadcast_to(value[:, s * TILE:(s + 1) * TILE], (TILE, TILE)).T
            column = jnp.concatenate([column, column], axis=1)
            for c in range(chunks):
                hit = place + float(c * 256) == column
                spread[p, s * TILE:(s + 1) * TILE, c * 256:(c + 1) * 256] = jnp.where(hit, 1.0, 0.0).astype(BF16)
        return 0

    rows_copy.wait()
    lax.fori_loop(0, n_nodes, prepare_pick, 0)

    pl.semaphore_wait(barrier, n_feat - 1 + n_nodes - 1)

    def copy_to_feat(source, target, sends, receives, shift):
        return pltpu.make_async_remote_copy(
            src_ref=source, dst_ref=target, send_sem=sends, recv_sem=receives,
            device_id=(me_q, feat_peer(shift)), device_id_type=MESH,
        )

    lines = ([(0, 2), (0, 1), (0, 3)], [(2, 0), (1, 0), (3, 0)])
    place_of = ((me_z, me_y), (me_y, me_z))

    def send_direct():
        for shift in feat_shifts:
            copy_to_feat(ag_send, ag_recv.at[me_f], ag_ss.at[0], ag_rs.at[0], shift).start()
        started_feat.append((ag_ss.at[0], ag_recv.at[pl.ds(0, n_feat - 1)]))

    def send_lines(a):
        for w in range(2):
            first, second = place_of[w]
            for shift in lines[w]:
                copy_to_feat(
                    line_send.at[a - 1, w], line_recv.at[a - 1, w, first, second],
                    line_ss.at[a, w], line_rs.at[a, w], shift,
                ).start()
            started_feat.append((line_ss.at[a, w], line_recv.at[a - 1, w, 0, pl.ds(0, 3)]))

    def relay_lines(a):
        for w in range(2):
            here = line_recv.at[a - 1, w, 0, pl.ds(0, 3)]
            copy_to_feat(here, here, line_ss.at[a, w], line_rs.at[a, w], (0, 1)).wait_recv()
            first = place_of[w][0]
            for shift in lines[1 - w]:
                copy_to_feat(
                    line_recv.at[a - 1, w, first], line_recv.at[a - 1, w, first],
                    line_ss.at[a, 2 + w], line_rs.at[a, 2 + w], shift,
                ).start()
            started_feat.append((line_ss.at[a, 2 + w], line_recv.at[a - 1, w, pl.ds(0, 3)]))

    send_direct()
    for a in range(1, 4):
        send_lines(a)

    def take_gathered(a):
        ref, group, target = gathered[a]
        if a == 0:
            here = ag_recv.at[pl.ds(0, n_feat - 1)]
            copy_to_feat(here, here, ag_ss.at[0], ag_rs.at[0], (0, 1)).wait_recv()
            for f in range(n_feat):
                got = ag_recv[f].astype(F32)
                target[f * width:(f + 1) * width, :half] = got[:width]
                target[f * width:(f + 1) * width, half:] = got[width:]
        else:
            quarter = half // 2
            for w in range(2):
                here = line_recv.at[a - 1, w, pl.ds(0, 3)]
                copy_to_feat(here, here, line_ss.at[a, 2 + w], line_rs.at[a, 2 + w], (0, 1)).wait_recv()
                for f in range(n_feat):
                    z, y = f // 4, f % 4
                    got = line_recv[a - 1, w, (z, y)[w], (y, z)[w]].astype(F32)
                    at = w * quarter
                    target[f * width:(f + 1) * width, at:at + quarter] = got[:width]
                    target[f * width:(f + 1) * width, half + at:half + at + quarter] = got[width:]
        target[pl.ds(pl.multiple_of(me_f * width, width), width), :] = ref[group]

    def lanes(c, size=256):
        return pl.ds(pl.multiple_of(c * size, size), size)

    def copy_to_node(source, target, sends, receives, shift):
        return pltpu.make_async_remote_copy(
            src_ref=source, dst_ref=target, send_sem=sends, recv_sem=receives,
            device_id=(node_peer(shift), me_f), device_id_type=MESH,
        )

    def forward(b, layer, group, u, with_gate=False):
        def step(c, _):
            states = u[:, lanes(c)]
            center = jnp.sum(states, axis=0, keepdims=True) * (1.0 / total)
            square = jnp.sum(states * states, axis=0, keepdims=True) * (1.0 / total)
            inv = lax.rsqrt(square - center * center + EPS)
            norm = (states - center) * inv
            gate = 1.0 / (1.0 + jnp.exp(-norm))
            normed[b, :, lanes(c)] = norm
            inverse[b, :, lanes(c)] = inv
            act = (norm * gate).astype(BF16)
            activ[b, :, lanes(c)] = act
            if with_gate:
                dgate[b, :, lanes(c)] = gate * (1.0 + norm * (1.0 - gate))
            value = dot(wt[layer, group], act).astype(BF16)
            mixed[:, lanes(c)] = value
            src[b][2 * c] = value[:, :TILE]
            src[b][2 * c + 1] = value[:, TILE:]
            return 0

        lax.fori_loop(0, chunks, step, 0, unroll=8)

    def aggregate(b, u):
        def step(t, _):
            tiles = [src[b][source_ref[k, t]] for k in range(depth)]
            u[:, lanes(t, TILE)] += dot(jnp.concatenate(tiles, axis=1), fwd_tiles[t])
            return 0

        lax.fori_loop(0, blocks, step, 0, unroll=16)

    def gates(b):
        def step(c, _):
            norm = normed[b, :, lanes(c)]
            gate = 1.0 / (1.0 + jnp.exp(-norm))
            dgate[b, :, lanes(c)] = gate * (1.0 + norm * (1.0 - gate))
            return 0

        lax.fori_loop(0, chunks, step, 0)

    def halo_send(b):
        for n, shift in enumerate(node_shifts):
            p = node_peer(shift)
            value = dot(mixed[...], pick[p]).astype(BF16)
            halo_out[b, p, 0] = value[:, :TILE]
            halo_out[b, p, 1] = value[:, TILE:]
            copy_to_node(
                halo_out.at[b, p], src[b].at[pl.ds(blocks + 2 * me_q, 2)], h_ss.at[b], h_rs.at[b, n // 2], shift
            ).start()
        started.append((h_ss.at[b], src[b].at[pl.ds(blocks, 2 * (n_nodes - 1))]))
        value = dot(mixed[...], pick[me_q]).astype(BF16)
        src[b][blocks + 2 * me_q] = value[:, :TILE]
        src[b][blocks + 2 * me_q + 1] = value[:, TILE:]

    def halo_wait(b, parts=range(4)):
        for n in parts:
            here = src[b].at[pl.ds(blocks, 2 if n == 3 else 4)]
            copy_to_node(here, here, h_ss.at[b], h_rs.at[b, n], mate).wait_recv()

    def lower(g):
        def step(t, _):
            low[t] = g[:, lanes(t, TILE)].astype(BF16)
            return 0

        lax.fori_loop(0, blocks, step, 0)

    def terms():
        segs[0] = jnp.zeros((total, TILE), F32)

        def step(j, _):
            acc = segs[TERM_UNROLL * j]
            for n in range(TERM_UNROLL):
                i = TERM_UNROLL * j + n
                part = dot(low[lax.rem(plan[0, i], blocks)], adj_sorted[i])
                acc = part + plan[1, i].astype(F32) * acc
                segs[i + 1] = acc
            return 0

        lax.fori_loop(0, slots // TERM_UNROLL, step, 0)

    def rim_send(b, early_rows=False):
        def rim(p):
            tiles = [segs[plan[2, blocks + 2 * p + s]] for s in range(2)]
            return jnp.concatenate(tiles, axis=1).astype(BF16)

        rows16 = pl.ds(pl.multiple_of(lax.div(me_f, 2) * 2 * width, 2 * width), 2 * width)
        for n, shift in enumerate(node_shifts):
            p = node_peer(shift)
            rim_out[b, p] = rim(p)
            if early_rows:
                copy_to_node(rim_out.at[b, p, rows16], own_in.at[me_q], own_sems.at[0], own_sems.at[1], shift).start()
        for n, shift in enumerate(node_shifts):
            p = node_peer(shift)
            copy_to_node(
                rim_out.at[b, p], rim_in.at[b, me_q], r_ss.at[b], r_rs.at[b, n // 2], shift
            ).start()
        if early_rows:
            started.append((own_sems.at[0], own_in.at[pl.ds(0, n_nodes - 1)]))
        started.append((r_ss.at[b], rim_in.at[b, pl.ds(0, n_nodes - 1)]))
        own = rim(me_q)

        def local(c, _):
            tiles = [segs[plan[2, 2 * c + h]] for h in range(2)]
            gm[:, lanes(c)] = jnp.concatenate(tiles, axis=1) + dot(own, spread[me_q, :, lanes(c)])
            return 0

        lax.fori_loop(0, chunks, local, 0, unroll=2)

    def rim_wait(b, n):
        here = rim_in.at[b, pl.ds(0, 1 if n == 3 else 2)]
        copy_to_node(here, here, r_ss.at[b], r_rs.at[b, n], mate).wait_recv()

    def rim_add(b, n):
        rim_wait(b, n)
        peers = [node_peer(back(shift)) for shift in ([mate] if n == 3 else groups[n])]

        def step(c, _):
            acc = gm[:, lanes(c)]
            for p in peers:
                acc = acc + dot(rim_in[b, p], spread[p, :, lanes(c)])
            gm[:, lanes(c)] = acc
            return 0

        lax.fori_loop(0, chunks, step, 0, unroll=2)

    def pull_back(b, layer, group, g, last=True):
        if last:
            rim_wait(b, 2)
            peers = [node_peer(back(shift)) for shift in groups[2]]

        def step(c, _):
            acc = gm[:, lanes(c)]
            if last:
                for p in peers:
                    acc = acc + dot(rim_in[b, p], spread[p, :, lanes(c)])
            gml[:, lanes(c)] = acc.astype(BF16)
            return 0

        lax.fori_loop(0, chunks, step, 0, unroll=4)

        def second_step(c, _):
            gnorm = dot(weights_ref[layer, group], gml[:, lanes(c)]) * dgate[b, :, lanes(c)]
            norm = normed[b, :, lanes(c)]
            first = jnp.sum(gnorm, axis=0, keepdims=True) * (1.0 / total)
            second = jnp.sum(gnorm * norm, axis=0, keepdims=True) * (1.0 / total)
            state = g[:, lanes(c)] + inverse[b, :, lanes(c)] * (gnorm - first - norm * second)
            g[:, lanes(c)] = state
            state = state.astype(BF16)
            low[2 * c] = state[:, :TILE]
            low[2 * c + 1] = state[:, TILE:]
            return 0

        lax.fori_loop(0, chunks, second_step, 0, unroll=8)

    puts = []

    def put(source, target, n):
        copy = pltpu.make_async_copy(source, target, out_sems.at[n])
        copy.start()
        puts.append(copy)

    def early_weight_rows():
        here = own_in.at[pl.ds(0, n_nodes - 1)]
        copy_to_node(here, here, own_sems.at[0], own_sems.at[1], mate).wait_recv()
        rows16 = pl.ds(pl.multiple_of(lax.div(me_f, 2) * 2 * width, 2 * width), 2 * width)
        peers = [node_peer(shift) for shift in node_shifts]

        def step(c, _):
            acc = gm[rows16, lanes(c)]
            for p in peers:
                acc = acc + dot(own_in[p], spread[p, :, lanes(c)])
            gml16[:, lanes(c)] = acc.astype(BF16)
            return 0

        lax.fori_loop(0, chunks, step, 0, unroll=2)
        weight_send(0, gml16[...])

    def weight_send(b, own=None):
        if own is None:
            own = gml[pl.ds(pl.multiple_of(lax.div(me_f, 2) * 2 * width, 2 * width), 2 * width), :]
        part = dot_nt(own, activ[b])
        part = jnp.where(lax.rem(me_f, 2) == 0, part[:width], part[width:])
        gw_send[b] = part
        gw_recv[b, me_q] = part
        for shift in node_shifts:
            copy_to_node(gw_send.at[b], gw_recv.at[b, me_q], w_ss.at[b], w_rs.at[b], shift).start()

    def mine(ref):
        return ref[pl.ds(pl.multiple_of(me_f * width, width), width), :]

    take_gathered(0)
    forward(0, 0, 0, x2)
    halo_send(0)
    relay_lines(1)
    relay_lines(2)
    relay_lines(3)
    gates(0)
    take_gathered(1)
    halo_wait(0)
    aggregate(0, x1)

    forward(1, 0, 1, x1)
    halo_send(1)
    gates(1)
    take_gathered(2)
    lower(g2)
    terms()
    rim_send(3)
    halo_wait(1)
    aggregate(1, x2)

    forward(2, 1, 0, x2)
    halo_send(2)
    gates(2)
    take_gathered(3)
    rim_add(3, 3)
    rim_add(3, 0)
    rim_add(3, 1)
    rim_add(3, 2)
    halo_wait(2)
    aggregate(2, x1)

    forward(3, 1, 1, x1, with_gate=True)
    pull_back(3, 1, 1, g1, last=False)
    terms()
    rim_send(2)
    weight_send(3)
    halo_send(3)
    out_ref[0] = mine(x1)
    put(out_ref.at[0], out_hbm.at[0], 0)
    rim_add(2, 3)
    rim_add(2, 0)
    rim_add(2, 1)
    pull_back(2, 1, 0, g2)

    terms()
    rim_send(1)
    weight_send(2)
    halo_wait(3)
    aggregate(3, x2)
    out_ref[1] = mine(x2)
    put(out_ref.at[1], out_hbm.at[1], 1)
    rim_add(1, 3)
    rim_add(1, 0)
    rim_add(1, 1)
    pull_back(1, 0, 1, g1)

    terms()
    rim_send(0, early_rows=True)
    weight_send(1)
    sg_ref[0] = mine(g1)
    put(sg_ref.at[0], sg_hbm.at[0], 2)
    early_weight_rows()
    rim_add(0, 3)
    rim_add(0, 0)
    rim_add(0, 1)
    pull_back(0, 0, 0, g2)
    sg_ref[1] = mine(g2)
    put(sg_ref.at[1], sg_hbm.at[1], 3)

    for b in range(4):
        here = gw_recv.at[b, pl.ds(0, n_nodes - 1)]
        pltpu.make_async_remote_copy(
            src_ref=here, dst_ref=here, send_sem=w_ss.at[b], recv_sem=w_rs.at[b],
            device_id=(node_peer(mate), me_f), device_id_type=MESH,
        ).wait()
        summed = gw_recv[b, 0]
        for p in range(1, n_nodes):
            summed = summed + gw_recv[b, p]
        wg_ref[b // 2, b % 2] = summed
        if b == 3:
            put(wg_ref, wg_hbm, 4)
    for sends, here in started_feat:
        copy_to_feat(here, here, sends, ag_rs.at[0], (0, 1)).wait_send()
    for sends, here in started:
        copy_to_node(here, here, sends, w_rs.at[0], mate).wait_send()
    for copy in puts:
        copy.wait()


def hand_over(out, sg, wg, out_ref, sg_ref, wg_ref):
    out_ref[...] = out[...]
    sg_ref[...] = sg[...]
    wg_ref[...] = wg[...]


def solution(mesh):
    n_nodes, n_feat = mesh.shape["nodes"], mesh.shape["feat"]

    def body(node_states, weights, adj_tiles, tile_source, tile_count, send_rows, send_count, out_grads):
        groups, width, rows = node_states.shape
        total = width * n_feat
        blocks, depth = tile_source.shape
        slots = send_rows.shape[2]
        source_tiles = blocks + n_nodes * slots // TILE
        vmem = pl.BlockSpec(memory_space=pltpu.VMEM)
        smem = pl.BlockSpec(memory_space=pltpu.SMEM)
        hbm = pl.BlockSpec(memory_space=pl.ANY)
        dma = pltpu.SemaphoreType.DMA((4,))
        outs = pl.pallas_call(
            functools.partial(kernel, n_nodes, n_feat),
            out_shape=(
                jax.ShapeDtypeStruct(node_states.shape, F32),
                jax.ShapeDtypeStruct(out_grads.shape, F32),
                jax.ShapeDtypeStruct((2, 2, width, total), F32),
            ),
            in_specs=[hbm] * 5 + [smem] * 3,
            out_specs=(hbm,) * 3,
            scratch_shapes=[
                pltpu.VMEM(node_states.shape, F32),
                pltpu.VMEM(out_grads.shape, F32),
                pltpu.VMEM(weights.shape, BF16),
                pltpu.VMEM(send_rows.shape, jnp.int32),
                pltpu.VMEM(node_states.shape, F32),
                pltpu.VMEM(out_grads.shape, F32),
                pltpu.VMEM((2, 2, width, total), F32),
                pltpu.VMEM(adj_tiles.shape, BF16),
                pltpu.VMEM((8, TILE), jnp.int32),
                pltpu.SMEM((8, TILE), jnp.int32),
                pltpu.SemaphoreType.DMA((6,)),
                pltpu.VMEM((2 * width, rows // 2), BF16),
                pltpu.VMEM((n_feat, 2 * width, rows // 2), BF16),
                pltpu.VMEM((3, 2, 2 * width, rows // 4), BF16),
                pltpu.VMEM((3, 2, 4, n_feat // 4, 2 * width, rows // 4), BF16),
                pltpu.SemaphoreType.DMA((4, 4)),
                pltpu.SemaphoreType.DMA((4, 4)),
                pltpu.VMEM((total, rows), F32),
                pltpu.VMEM((total, rows), F32),
                pltpu.VMEM((total, rows), F32),
                pltpu.VMEM((total, rows), F32),
                pltpu.VMEM((2, 2, total, total), BF16),
                pltpu.VMEM((blocks, depth * TILE, TILE), BF16),
                pltpu.VMEM((blocks * depth, TILE, TILE), BF16),
                pltpu.VMEM((n_nodes, rows, slots), BF16),
                pltpu.VMEM((n_nodes, slots, rows), BF16),
                pltpu.VMEM((4, total, rows), F32),
                pltpu.VMEM((4, total, rows), F32),
                pltpu.VMEM((4, total, rows), BF16),
                pltpu.VMEM((4, 1, rows), F32),
                pltpu.VMEM((total, rows), BF16),
                *[pltpu.VMEM((source_tiles, total, TILE), BF16)] * 4,
                pltpu.VMEM((4, n_nodes, 2, total, TILE), BF16),
                pltpu.VMEM((blocks, total, TILE), BF16),
                pltpu.VMEM((blocks * depth + 1, total, TILE), F32),
                pltpu.VMEM((4, n_nodes, total, slots), BF16),
                pltpu.VMEM((4, n_nodes, total, slots), BF16),
                pltpu.VMEM((total, rows), F32),
                pltpu.VMEM((total, rows), BF16),
                pltpu.VMEM((4, width, total), F32),
                pltpu.VMEM((4, n_nodes, width, total), F32),
                pltpu.VMEM((n_nodes, 2 * width, slots), BF16),
                pltpu.VMEM((2 * width, rows), BF16),
                pltpu.SemaphoreType.DMA((5,)),
                dma, dma, dma, pltpu.SemaphoreType.DMA((4, 4)), dma, pltpu.SemaphoreType.DMA((4, 4)), dma, dma,
                pltpu.SemaphoreType.DMA((2,)),
            ],
            compiler_params=pltpu.CompilerParams(
                collective_id=0, has_side_effects=True, vmem_limit_bytes=62 * 2**20
            ),
        )(
            node_states, out_grads, weights, adj_tiles, send_rows,
            tile_source.T, tile_count, send_count,
        )
        outs = pl.pallas_call(
            hand_over,
            out_shape=tuple(jax.ShapeDtypeStruct(o.shape, o.dtype) for o in outs),
            in_specs=[vmem] * 3,
            out_specs=(vmem,) * 3,
        )(*outs)
        return outs[0], outs[1], jnp.swapaxes(outs[2], 2, 3)

    return jax.shard_map(
        body,
        mesh=mesh,
        in_specs=(
            P(None, "feat", "nodes"),
            P(),
            P("nodes", None, None, None),
            P("nodes", None),
            P("nodes"),
            P("nodes", None, None),
            P("nodes", None),
            P(None, "feat", "nodes"),
        ),
        out_specs=(P(None, "feat", "nodes"), P(None, "feat", "nodes"), P(None, None, None, "feat")),
        check_vma=False,
    )
```

```python
import functools

import jax
import jax.numpy as jnp
from jax import lax
from jax.experimental import pallas as pl
from jax.experimental.pallas import tpu as pltpu
from jax.sharding import PartitionSpec as P

MESH = pl.DeviceIdType.MESH
TILE = 128
EPS = 1e-05
TERM_UNROLL = 32
F32 = jnp.float32
BF16 = jnp.bfloat16


def dot(a, b):
    return jnp.dot(a, b, preferred_element_type=F32)


def dot_nt(a, b):
    return lax.dot_general(a, b, (((1,), (1,)), ((), ())), preferred_element_type=F32)


def kernel(
    n_nodes, n_feat,
    states_hbm, grads_hbm, weights_hbm, adj_hbm, rows_hbm,
    source_ref, count_ref, sent_ref,
    out_hbm, sg_hbm, wg_hbm,
    states_ref, grads_ref, weights_ref, rows_ref, out_ref, sg_ref, wg_ref,
    adj_ref, plan_rows, plan, local_sems,
    ag_send, ag_recv, line_send, line_recv, line_ss, line_rs, x1, x2, g1, g2, wt,
    fwd_tiles, adj_sorted, pick, spread,
    normed, dgate, activ, inverse, mixed,
    src0, src1, src2, src3, halo_out, low, segs, rim_out, rim_in, gm, gml,
    gw_send, gw_recv, own_in, gml16, out_sems,
    ag_ss, ag_rs, h_ss, h_rs, r_ss, r_rs, w_ss, w_rs, own_sems,
):
    src = (src0, src1, src2, src3)
    me_q = lax.axis_index("nodes")
    me_f = lax.axis_index("feat")
    width = states_ref.shape[1]
    rows = states_ref.shape[2]
    total = width * n_feat
    half = rows // 2
    blocks = rows // TILE
    chunks = rows // 256
    depth = adj_ref.shape[1]
    slots = blocks * depth

    me_x, me_c = lax.div(me_q, 2), lax.rem(me_q, 2)
    me_z, me_y = lax.div(me_f, 4), lax.rem(me_f, 4)

    def node_peer(shift):
        dx, dc = shift
        return lax.rem(me_x + dx, n_nodes // 2) * 2 + lax.rem(me_c + dc, 2)

    def feat_peer(shift):
        dz, dy = shift
        return lax.rem(me_z + dz, n_feat // 4) * 4 + lax.rem(me_y + dy, 4)

    def hops(shift):
        return min(shift[0], 4 - shift[0]) + min(shift[1], 4 - shift[1])

    feat_shifts = [(dz, dy) for dz in range(4) for dy in range(4) if dz or dy]
    feat_shifts.sort(key=lambda shift: -hops(shift))
    mate = (0, 1)
    groups = [((2, 0), (2, 1)), ((1, 0), (3, 0)), ((1, 1), (3, 1))]
    far_shifts = [shift for group in groups for shift in group]
    node_shifts = far_shifts + [mate]

    def back(shift):
        return ((4 - shift[0]) % 4, shift[1])

    started = []
    started_feat = []
    barrier = pltpu.get_barrier_semaphore()
    for shift in feat_shifts:
        pl.semaphore_signal(barrier, inc=1, device_id=(me_q, feat_peer(shift)), device_id_type=MESH)
    for shift in node_shifts:
        pl.semaphore_signal(barrier, inc=1, device_id=(node_peer(shift), me_f), device_id_type=MESH)

    states_copy = pltpu.make_async_copy(states_hbm, states_ref, local_sems.at[2])
    grads_copy = pltpu.make_async_copy(grads_hbm, grads_ref, local_sems.at[3])
    rows_copy = pltpu.make_async_copy(rows_hbm, rows_ref, local_sems.at[4])
    weights_copy = pltpu.make_async_copy(weights_hbm, weights_ref, local_sems.at[5])
    adj_copy = pltpu.make_async_copy(adj_hbm, adj_ref, local_sems.at[0])
    for copy in (states_copy, grads_copy, rows_copy, weights_copy, adj_copy):
        copy.start()
    states_copy.wait()
    grads_copy.wait()

    gathered = [(states_ref, 1, x2), (states_ref, 0, x1), (grads_ref, 1, g2), (grads_ref, 0, g1)]
    for a, (ref, group, _) in enumerate(gathered):
        packed = jnp.concatenate([ref[group, :, :half], ref[group, :, half:]], axis=0).astype(BF16)
        if a == 0:
            ag_send[...] = packed
            ag_recv[me_f] = packed
        else:
            quarter = half // 2
            line_send[a - 1, 0] = packed[:, :quarter]
            line_send[a - 1, 1] = packed[:, quarter:]
            line_recv[a - 1, 0, me_z, me_y] = packed[:, :quarter]
            line_recv[a - 1, 1, me_y, me_z] = packed[:, quarter:]
    weights_copy.wait()
    for layer in range(2):
        for group in range(2):
            wt[layer, group] = weights_ref[layer, group].astype(F32).T.astype(BF16)

    lane = lax.broadcasted_iota(jnp.int32, (1, TILE), 1)
    source = jnp.full((1, TILE), blocks * TILE, jnp.int32)
    for e in range(slots):
        source = jnp.where(lane == e, source_ref[e // blocks, e % blocks], source)
    place = lax.broadcasted_iota(jnp.int32, (TILE, TILE), 0)
    lanes_of = lax.broadcasted_iota(jnp.int32, (TILE, TILE), 1)

    def column(row):
        return jnp.broadcast_to(row, (TILE, TILE)).T

    source_column = column(source)
    key = source * TILE + lane
    rank = column(jnp.sum((column(key) < key).astype(jnp.int32), axis=0, keepdims=True))
    at = rank == lanes_of
    before = rank + 1 == lanes_of
    order = jnp.sum(jnp.where(at, place, 0), axis=0, keepdims=True)
    ordered = jnp.sum(jnp.where(at, source_column, 0), axis=0, keepdims=True)
    previous = jnp.sum(jnp.where(before, source_column, 0), axis=0, keepdims=True)
    keep = jnp.where((ordered == previous) & (lane > 0), 1, 0)
    upto = jnp.sum((source_column <= lanes_of).astype(jnp.int32), axis=0, keepdims=True)
    has = jnp.sum((source_column == lanes_of).astype(jnp.int32), axis=0, keepdims=True)
    plan_rows[0:1, :] = order
    plan_rows[1:2, :] = keep
    plan_rows[2:3, :] = jnp.where(has > 0, upto, 0)
    plan_copy = pltpu.make_async_copy(plan_rows, plan, local_sems.at[1])
    plan_copy.start()

    def prepare_block(t, _):
        for k in range(depth):
            keep = (k < count_ref[t]).astype(F32)
            tile = adj_ref[t, k].astype(F32) * keep
            fwd_tiles[t, k * TILE:(k + 1) * TILE, :] = tile.T.astype(BF16)
        return 0

    adj_copy.wait()
    lax.fori_loop(0, blocks, prepare_block, 0)

    def prepare_sorted(i, _):
        e = plan[0, i]
        t = lax.rem(e, blocks)
        k = lax.div(e, blocks)
        keep = (k < count_ref[t]).astype(F32)
        adj_sorted[i] = (adj_ref[t, k].astype(F32) * keep).astype(BF16)
        return 0

    plan_copy.wait()
    lax.fori_loop(0, slots, prepare_sorted, 0)

    def prepare_pick(p, _):
        lane = lax.broadcasted_iota(jnp.int32, (1, 256), 1)
        index = jnp.where(lane < sent_ref[0, p], rows_ref[0, pl.ds(p, 1), :], -1)
        high = lax.broadcasted_iota(jnp.int32, (256, 256), 0)
        for c in range(chunks):
            hit = high + c * 256 == index
            pick[p, c * 256:(c + 1) * 256, :] = jnp.where(hit, 1.0, 0.0).astype(BF16)
        value = index.astype(F32)
        place = lax.broadcasted_iota(jnp.int32, (TILE, 256), 1).astype(F32)
        for s in range(2):
            column = jnp.broadcast_to(value[:, s * TILE:(s + 1) * TILE], (TILE, TILE)).T
            column = jnp.concatenate([column, column], axis=1)
            for c in range(chunks):
                hit = place + float(c * 256) == column
                spread[p, s * TILE:(s + 1) * TILE, c * 256:(c + 1) * 256] = jnp.where(hit, 1.0, 0.0).astype(BF16)
        return 0

    rows_copy.wait()
    lax.fori_loop(0, n_nodes, prepare_pick, 0)

    pl.semaphore_wait(barrier, n_feat - 1 + n_nodes - 1)

    def copy_to_feat(source, target, sends, receives, shift):
        return pltpu.make_async_remote_copy(
            src_ref=source, dst_ref=target, send_sem=sends, recv_sem=receives,
            device_id=(me_q, feat_peer(shift)), device_id_type=MESH,
        )

    lines = ([(0, 2), (0, 1), (0, 3)], [(2, 0), (1, 0), (3, 0)])
    place_of = ((me_z, me_y), (me_y, me_z))

    def send_direct():
        for shift in feat_shifts:
            copy_to_feat(ag_send, ag_recv.at[me_f], ag_ss.at[0], ag_rs.at[0], shift).start()
        started_feat.append((ag_ss.at[0], ag_recv.at[pl.ds(0, n_feat - 1)]))

    def send_lines(a):
        for w in range(2):
            first, second = place_of[w]
            for shift in lines[w]:
                copy_to_feat(
                    line_send.at[a - 1, w], line_recv.at[a - 1, w, first, second],
                    line_ss.at[a, w], line_rs.at[a, w], shift,
                ).start()
            started_feat.append((line_ss.at[a, w], line_recv.at[a - 1, w, 0, pl.ds(0, 3)]))

    def relay_lines(a):
        for w in range(2):
            here = line_recv.at[a - 1, w, 0, pl.ds(0, 3)]
            copy_to_feat(here, here, line_ss.at[a, w], line_rs.at[a, w], (0, 1)).wait_recv()
            first = place_of[w][0]
            for shift in lines[1 - w]:
                copy_to_feat(
                    line_recv.at[a - 1, w, first], line_recv.at[a - 1, w, first],
                    line_ss.at[a, 2 + w], line_rs.at[a, 2 + w], shift,
                ).start()
            started_feat.append((line_ss.at[a, 2 + w], line_recv.at[a - 1, w, pl.ds(0, 3)]))

    send_direct()
    for a in range(1, 4):
        send_lines(a)

    def take_gathered(a):
        ref, group, target = gathered[a]
        if a == 0:
            here = ag_recv.at[pl.ds(0, n_feat - 1)]
            copy_to_feat(here, here, ag_ss.at[0], ag_rs.at[0], (0, 1)).wait_recv()
            for f in range(n_feat):
                got = ag_recv[f].astype(F32)
                target[f * width:(f + 1) * width, :half] = got[:width]
                target[f * width:(f + 1) * width, half:] = got[width:]
        else:
            quarter = half // 2
            for w in range(2):
                here = line_recv.at[a - 1, w, pl.ds(0, 3)]
                copy_to_feat(here, here, line_ss.at[a, 2 + w], line_rs.at[a, 2 + w], (0, 1)).wait_recv()
                for f in range(n_feat):
                    z, y = f // 4, f % 4
                    got = line_recv[a - 1, w, (z, y)[w], (y, z)[w]].astype(F32)
                    at = w * quarter
                    target[f * width:(f + 1) * width, at:at + quarter] = got[:width]
                    target[f * width:(f + 1) * width, half + at:half + at + quarter] = got[width:]
        target[pl.ds(pl.multiple_of(me_f * width, width), width), :] = ref[group]

    def lanes(c, size=256):
        return pl.ds(pl.multiple_of(c * size, size), size)

    def copy_to_node(source, target, sends, receives, shift):
        return pltpu.make_async_remote_copy(
            src_ref=source, dst_ref=target, send_sem=sends, recv_sem=receives,
            device_id=(node_peer(shift), me_f), device_id_type=MESH,
        )

    def forward(b, layer, group, u, with_gate=False):
        def step(c, _):
            states = u[:, lanes(c)]
            center = jnp.sum(states, axis=0, keepdims=True) * (1.0 / total)
            square = jnp.sum(states * states, axis=0, keepdims=True) * (1.0 / total)
            inv = lax.rsqrt(square - center * center + EPS)
            norm = (states - center) * inv
            gate = 1.0 / (1.0 + jnp.exp(-norm))
            normed[b, :, lanes(c)] = norm
            inverse[b, :, lanes(c)] = inv
            act = (norm * gate).astype(BF16)
            activ[b, :, lanes(c)] = act
            if with_gate:
                dgate[b, :, lanes(c)] = gate * (1.0 + norm * (1.0 - gate))
            value = dot(wt[layer, group], act).astype(BF16)
            mixed[:, lanes(c)] = value
            src[b][2 * c] = value[:, :TILE]
            src[b][2 * c + 1] = value[:, TILE:]
            return 0

        lax.fori_loop(0, chunks, step, 0, unroll=8)

    def aggregate(b, u):
        def step(t, _):
            tiles = [src[b][source_ref[k, t]] for k in range(depth)]
            u[:, lanes(t, TILE)] += dot(jnp.concatenate(tiles, axis=1), fwd_tiles[t])
            return 0

        lax.fori_loop(0, blocks, step, 0, unroll=16)

    def gates(b):
        def step(c, _):
            norm = normed[b, :, lanes(c)]
            gate = 1.0 / (1.0 + jnp.exp(-norm))
            dgate[b, :, lanes(c)] = gate * (1.0 + norm * (1.0 - gate))
            return 0

        lax.fori_loop(0, chunks, step, 0)

    def halo_send(b):
        for n, shift in enumerate(node_shifts):
            p = node_peer(shift)
            value = dot(mixed[...], pick[p]).astype(BF16)
            halo_out[b, p, 0] = value[:, :TILE]
            halo_out[b, p, 1] = value[:, TILE:]
            copy_to_node(
                halo_out.at[b, p], src[b].at[pl.ds(blocks + 2 * me_q, 2)], h_ss.at[b], h_rs.at[b, n // 2], shift
            ).start()
        started.append((h_ss.at[b], src[b].at[pl.ds(blocks, 2 * (n_nodes - 1))]))
        value = dot(mixed[...], pick[me_q]).astype(BF16)
        src[b][blocks + 2 * me_q] = value[:, :TILE]
        src[b][blocks + 2 * me_q + 1] = value[:, TILE:]

    def halo_wait(b, parts=range(4)):
        for n in parts:
            here = src[b].at[pl.ds(blocks, 2 if n == 3 else 4)]
            copy_to_node(here, here, h_ss.at[b], h_rs.at[b, n], mate).wait_recv()

    def lower(g):
        def step(t, _):
            low[t] = g[:, lanes(t, TILE)].astype(BF16)
            return 0

        lax.fori_loop(0, blocks, step, 0)

    def terms():
        segs[0] = jnp.zeros((total, TILE), F32)

        def step(j, _):
            acc = segs[TERM_UNROLL * j]
            for n in range(TERM_UNROLL):
                i = TERM_UNROLL * j + n
                part = dot(low[lax.rem(plan[0, i], blocks)], adj_sorted[i])
                acc = part + plan[1, i].astype(F32) * acc
                segs[i + 1] = acc
            return 0

        lax.fori_loop(0, slots // TERM_UNROLL, step, 0)

    def rim_send(b, early_rows=False):
        def rim(p):
            tiles = [segs[plan[2, blocks + 2 * p + s]] for s in range(2)]
            return jnp.concatenate(tiles, axis=1).astype(BF16)

        rows16 = pl.ds(pl.multiple_of(lax.div(me_f, 2) * 2 * width, 2 * width), 2 * width)
        for n, shift in enumerate(node_shifts):
            p = node_peer(shift)
            rim_out[b, p] = rim(p)
            if early_rows:
                copy_to_node(rim_out.at[b, p, rows16], own_in.at[me_q], own_sems.at[0], own_sems.at[1], shift).start()
        for n, shift in enumerate(node_shifts):
            p = node_peer(shift)
            copy_to_node(
                rim_out.at[b, p], rim_in.at[b, me_q], r_ss.at[b], r_rs.at[b, n // 2], shift
            ).start()
        if early_rows:
            started.append((own_sems.at[0], own_in.at[pl.ds(0, n_nodes - 1)]))
        started.append((r_ss.at[b], rim_in.at[b, pl.ds(0, n_nodes - 1)]))
        own = rim(me_q)

        def local(c, _):
            tiles = [segs[plan[2, 2 * c + h]] for h in range(2)]
            gm[:, lanes(c)] = jnp.concatenate(tiles, axis=1) + dot(own, spread[me_q, :, lanes(c)])
            return 0

        lax.fori_loop(0, chunks, local, 0, unroll=4)

    def rim_wait(b, n):
        here = rim_in.at[b, pl.ds(0, 1 if n == 3 else 2)]
        copy_to_node(here, here, r_ss.at[b], r_rs.at[b, n], mate).wait_recv()

    def rim_add(b, n):
        rim_wait(b, n)
        peers = [node_peer(back(shift)) for shift in ([mate] if n == 3 else groups[n])]

        def step(c, _):
            acc = gm[:, lanes(c)]
            for p in peers:
                acc = acc + dot(rim_in[b, p], spread[p, :, lanes(c)])
            gm[:, lanes(c)] = acc
            return 0

        lax.fori_loop(0, chunks, step, 0, unroll=4)

    def pull_back(b, layer, group, g, last=True):
        if last:
            rim_wait(b, 2)
            peers = [node_peer(back(shift)) for shift in groups[2]]

        def step(c, _):
            acc = gm[:, lanes(c)]
            if last:
                for p in peers:
                    acc = acc + dot(rim_in[b, p], spread[p, :, lanes(c)])
            gml[:, lanes(c)] = acc.astype(BF16)
            return 0

        lax.fori_loop(0, chunks, step, 0, unroll=4)

        def second_step(c, _):
            gnorm = dot(weights_ref[layer, group], gml[:, lanes(c)]) * dgate[b, :, lanes(c)]
            norm = normed[b, :, lanes(c)]
            first = jnp.sum(gnorm, axis=0, keepdims=True) * (1.0 / total)
            second = jnp.sum(gnorm * norm, axis=0, keepdims=True) * (1.0 / total)
            state = g[:, lanes(c)] + inverse[b, :, lanes(c)] * (gnorm - first - norm * second)
            g[:, lanes(c)] = state
            state = state.astype(BF16)
            low[2 * c] = state[:, :TILE]
            low[2 * c + 1] = state[:, TILE:]
            return 0

        lax.fori_loop(0, chunks, second_step, 0, unroll=8)

    puts = []

    def put(source, target, n):
        copy = pltpu.make_async_copy(source, target, out_sems.at[n])
        copy.start()
        puts.append(copy)

    def early_weight_rows():
        here = own_in.at[pl.ds(0, n_nodes - 1)]
        copy_to_node(here, here, own_sems.at[0], own_sems.at[1], mate).wait_recv()
        rows16 = pl.ds(pl.multiple_of(lax.div(me_f, 2) * 2 * width, 2 * width), 2 * width)
        peers = [node_peer(shift) for shift in node_shifts]

        def step(c, _):
            acc = gm[rows16, lanes(c)]
            for p in peers:
                acc = acc + dot(own_in[p], spread[p, :, lanes(c)])
            gml16[:, lanes(c)] = acc.astype(BF16)
            return 0

        lax.fori_loop(0, chunks, step, 0, unroll=4)
        weight_send(0, gml16[...])

    def weight_send(b, own=None):
        if own is None:
            own = gml[pl.ds(pl.multiple_of(lax.div(me_f, 2) * 2 * width, 2 * width), 2 * width), :]
        part = dot_nt(own, activ[b])
        part = jnp.where(lax.rem(me_f, 2) == 0, part[:width], part[width:])
        gw_send[b] = part
        gw_recv[b, me_q] = part
        for shift in node_shifts:
            copy_to_node(gw_send.at[b], gw_recv.at[b, me_q], w_ss.at[b], w_rs.at[b], shift).start()

    def mine(ref):
        return ref[pl.ds(pl.multiple_of(me_f * width, width), width), :]

    take_gathered(0)
    forward(0, 0, 0, x2)
    halo_send(0)
    relay_lines(1)
    relay_lines(2)
    relay_lines(3)
    gates(0)
    take_gathered(1)
    halo_wait(0)
    aggregate(0, x1)

    forward(1, 0, 1, x1)
    halo_send(1)
    gates(1)
    take_gathered(2)
    lower(g2)
    terms()
    rim_send(3)
    halo_wait(1)
    aggregate(1, x2)

    forward(2, 1, 0, x2)
    halo_send(2)
    gates(2)
    take_gathered(3)
    rim_add(3, 3)
    rim_add(3, 0)
    rim_add(3, 1)
    rim_add(3, 2)
    halo_wait(2)
    aggregate(2, x1)

    forward(3, 1, 1, x1, with_gate=True)
    pull_back(3, 1, 1, g1, last=False)
    terms()
    rim_send(2)
    weight_send(3)
    halo_send(3)
    out_ref[0] = mine(x1)
    put(out_ref.at[0], out_hbm.at[0], 0)
    rim_add(2, 3)
    rim_add(2, 0)
    rim_add(2, 1)
    pull_back(2, 1, 0, g2)

    terms()
    rim_send(1)
    weight_send(2)
    halo_wait(3)
    aggregate(3, x2)
    out_ref[1] = mine(x2)
    put(out_ref.at[1], out_hbm.at[1], 1)
    rim_add(1, 3)
    rim_add(1, 0)
    rim_add(1, 1)
    pull_back(1, 0, 1, g1)

    terms()
    rim_send(0, early_rows=True)
    weight_send(1)
    sg_ref[0] = mine(g1)
    put(sg_ref.at[0], sg_hbm.at[0], 2)
    early_weight_rows()
    rim_add(0, 3)
    rim_add(0, 0)
    rim_add(0, 1)
    pull_back(0, 0, 0, g2)
    sg_ref[1] = mine(g2)
    put(sg_ref.at[1], sg_hbm.at[1], 3)

    for b in range(4):
        here = gw_recv.at[b, pl.ds(0, n_nodes - 1)]
        pltpu.make_async_remote_copy(
            src_ref=here, dst_ref=here, send_sem=w_ss.at[b], recv_sem=w_rs.at[b],
            device_id=(node_peer(mate), me_f), device_id_type=MESH,
        ).wait()
        summed = gw_recv[b, 0]
        for p in range(1, n_nodes):
            summed = summed + gw_recv[b, p]
        wg_ref[b // 2, b % 2] = summed
        if b == 3:
            put(wg_ref, wg_hbm, 4)
    for sends, here in started_feat:
        copy_to_feat(here, here, sends, ag_rs.at[0], (0, 1)).wait_send()
    for sends, here in started:
        copy_to_node(here, here, sends, w_rs.at[0], mate).wait_send()
    for copy in puts:
        copy.wait()


def hand_over(out, sg, wg, out_ref, sg_ref, wg_ref):
    out_ref[...] = out[...]
    sg_ref[...] = sg[...]
    wg_ref[...] = wg[...]


def solution(mesh):
    n_nodes, n_feat = mesh.shape["nodes"], mesh.shape["feat"]

    def body(node_states, weights, adj_tiles, tile_source, tile_count, send_rows, send_count, out_grads):
        groups, width, rows = node_states.shape
        total = width * n_feat
        blocks, depth = tile_source.shape
        slots = send_rows.shape[2]
        source_tiles = blocks + n_nodes * slots // TILE
        vmem = pl.BlockSpec(memory_space=pltpu.VMEM)
        smem = pl.BlockSpec(memory_space=pltpu.SMEM)
        hbm = pl.BlockSpec(memory_space=pl.ANY)
        dma = pltpu.SemaphoreType.DMA((4,))
        outs = pl.pallas_call(
            functools.partial(kernel, n_nodes, n_feat),
            out_shape=(
                jax.ShapeDtypeStruct(node_states.shape, F32),
                jax.ShapeDtypeStruct(out_grads.shape, F32),
                jax.ShapeDtypeStruct((2, 2, width, total), F32),
            ),
            in_specs=[hbm] * 5 + [smem] * 3,
            out_specs=(hbm,) * 3,
            scratch_shapes=[
                pltpu.VMEM(node_states.shape, F32),
                pltpu.VMEM(out_grads.shape, F32),
                pltpu.VMEM(weights.shape, BF16),
                pltpu.VMEM(send_rows.shape, jnp.int32),
                pltpu.VMEM(node_states.shape, F32),
                pltpu.VMEM(out_grads.shape, F32),
                pltpu.VMEM((2, 2, width, total), F32),
                pltpu.VMEM(adj_tiles.shape, BF16),
                pltpu.VMEM((8, TILE), jnp.int32),
                pltpu.SMEM((8, TILE), jnp.int32),
                pltpu.SemaphoreType.DMA((6,)),
                pltpu.VMEM((2 * width, rows // 2), BF16),
                pltpu.VMEM((n_feat, 2 * width, rows // 2), BF16),
                pltpu.VMEM((3, 2, 2 * width, rows // 4), BF16),
                pltpu.VMEM((3, 2, 4, n_feat // 4, 2 * width, rows // 4), BF16),
                pltpu.SemaphoreType.DMA((4, 4)),
                pltpu.SemaphoreType.DMA((4, 4)),
                pltpu.VMEM((total, rows), F32),
                pltpu.VMEM((total, rows), F32),
                pltpu.VMEM((total, rows), F32),
                pltpu.VMEM((total, rows), F32),
                pltpu.VMEM((2, 2, total, total), BF16),
                pltpu.VMEM((blocks, depth * TILE, TILE), BF16),
                pltpu.VMEM((blocks * depth, TILE, TILE), BF16),
                pltpu.VMEM((n_nodes, rows, slots), BF16),
                pltpu.VMEM((n_nodes, slots, rows), BF16),
                pltpu.VMEM((4, total, rows), F32),
                pltpu.VMEM((4, total, rows), F32),
                pltpu.VMEM((4, total, rows), BF16),
                pltpu.VMEM((4, 1, rows), F32),
                pltpu.VMEM((total, rows), BF16),
                *[pltpu.VMEM((source_tiles, total, TILE), BF16)] * 4,
                pltpu.VMEM((4, n_nodes, 2, total, TILE), BF16),
                pltpu.VMEM((blocks, total, TILE), BF16),
                pltpu.VMEM((blocks * depth + 1, total, TILE), F32),
                pltpu.VMEM((4, n_nodes, total, slots), BF16),
                pltpu.VMEM((4, n_nodes, total, slots), BF16),
                pltpu.VMEM((total, rows), F32),
                pltpu.VMEM((total, rows), BF16),
                pltpu.VMEM((4, width, total), F32),
                pltpu.VMEM((4, n_nodes, width, total), F32),
                pltpu.VMEM((n_nodes, 2 * width, slots), BF16),
                pltpu.VMEM((2 * width, rows), BF16),
                pltpu.SemaphoreType.DMA((5,)),
                dma, dma, dma, pltpu.SemaphoreType.DMA((4, 4)), dma, pltpu.SemaphoreType.DMA((4, 4)), dma, dma,
                pltpu.SemaphoreType.DMA((2,)),
            ],
            compiler_params=pltpu.CompilerParams(
                collective_id=0, has_side_effects=True, vmem_limit_bytes=62 * 2**20
            ),
        )(
            node_states, out_grads, weights, adj_tiles, send_rows,
            tile_source.T, tile_count, send_count,
        )
        outs = pl.pallas_call(
            hand_over,
            out_shape=tuple(jax.ShapeDtypeStruct(o.shape, o.dtype) for o in outs),
            in_specs=[vmem] * 3,
            out_specs=(vmem,) * 3,
        )(*outs)
        return outs[0], outs[1], jnp.swapaxes(outs[2], 2, 3)

    return jax.shard_map(
        body,
        mesh=mesh,
        in_specs=(
            P(None, "feat", "nodes"),
            P(),
            P("nodes", None, None, None),
            P("nodes", None),
            P("nodes"),
            P("nodes", None, None),
            P("nodes", None),
            P(None, "feat", "nodes"),
        ),
        out_specs=(P(None, "feat", "nodes"), P(None, "feat", "nodes"), P(None, None, None, "feat")),
        check_vma=False,
    )
```
